128 devices in a mesh: row: 8 (over x_hi, z), col: 16 (over x_lo, y, core).
Axes of the slice: x: 4 (x_hi: 2, x_lo: 2; x = x_hi * 2 + x_lo), y: 4, z: 4, core: 2. Of those that a mesh axis runs over, the one named last changes fastest.
Arguments:
- pair_rep: float32 [384, 384, 128], P('row', 'col'), may hold values from -24 to 24
- chain_id: int32 [384], replicated, may hold values from 0 to 3, never falling along the last dimension, each value on 1 to 192 neighbouring positions
- live_mask: int32 [384], replicated, may hold values from 0 to 1, as said below
- chain_table: float32 [2, 128], replicated, may hold values from -4 to 4
- tri_proj: bfloat16 [2, 128, 512], replicated, may hold values from -0.5 to 0.5
- tri_gate: bfloat16 [2, 128, 128], replicated, may hold values from -0.5 to 0.5
- tri_out: bfloat16 [2, 128, 128], replicated, may hold values from -0.5 to 0.5
- att_project: bfloat16 [2, 128, 512], replicated, may hold values from -0.5 to 0.5
- att_bias: float32 [2, 128, 4], replicated, may hold values from -20 to 20
- att_out: bfloat16 [2, 128, 128], replicated, may hold values from -0.5 to 0.5
Outputs:
- pair_out: float32 [384, 384, 128], P('row', 'col')
The draws below stay inside these ranges and needn't reach their ends.
Inputs may be any that keep to these rules, and one draw needn't show every extreme that they name: chain_id never falls along the residues, and each of the 4 chains holds at least one residue. live_mask is 1 on the first residues and 0 on the rest; at least 192 residues are live.
All inputs are finite; a program needn't handle non-finite values.
Results may differ from the reference program's by a relative error of at most 0.0075.
Values may be sent and summed in bfloat16 or wider, within the bound.
A program may use at most 128 MiB of HBM per device.

```python
import math
import jax
import jax.numpy as jnp
import numpy as np
from jax import lax

CZ = 128
CH = 128
HEADS = 4
DH = 32
CHAINS = 4
RES_COL = 24
NRES = 384


def draw_pair_rep(key, part):
    key = jax.random.fold_in(key, 11)
    keys = jax.random.split(key, 3)
    channel_scale = 0.3 * jnp.exp(jax.random.uniform(keys[0], (CZ,), jnp.float32, 0.0, math.log(10.0)))
    cell_scale = jnp.exp(jax.random.uniform(keys[1], (NRES, NRES, 1), jnp.float32, math.log(0.5), math.log(2.0)))
    base_values = jnp.clip(jax.random.normal(keys[2], (NRES, NRES, CZ), jnp.float32), -4.0, 4.0)
    return base_values * channel_scale * cell_scale


def draw_live_mask(key, part):
    key = jax.random.fold_in(key, 12)
    live_count = jax.random.randint(key, (), NRES // 2, NRES + 1)
    return (jnp.arange(NRES, dtype=jnp.int32) < live_count).astype(jnp.int32)


def draw_att_bias(key, part):
    key = jax.random.fold_in(key, 13)
    base_values = jnp.clip(jax.random.normal(key, (2, CZ, HEADS), jnp.float32), -4.0, 4.0)
    return 2.0 * base_values / math.sqrt(CZ)


def profile(number_of, total, most, slope):
    weights = [(1 << 20) // math.isqrt(grade ** slope) + 1 for grade in range(2, number_of + 1)]
    rest, holding = total - most - (number_of - 1), [1] * (number_of - 1)
    while rest > 0:
        candidates = [i for i in range(number_of - 1) if holding[i] < most]
        pool, remaining = sum([weights[i] for i in candidates]), rest
        for i in candidates:
            addition = min(most - holding[i], max(1, remaining * weights[i] // pool), rest)
            holding[i] = holding[i] + addition
            rest = rest - addition
    return np.array([most] + holding)


def uneven_parts(key, count, total, bound, skew):
    if count == 2:
        one = jax.random.randint(key, (), max(1, total - bound), min(bound, total - 1) + 1)
        return jnp.stack([one, total - one])
    lengths = jnp.asarray(profile(count, total, bound, skew), jnp.int32)
    pairs = (count - 1) // 2
    donor, sink = lengths[1:1 + 2 * pairs:2], lengths[2:2 + 2 * pairs:2]
    slack = jnp.minimum(donor - 1, bound - sink)
    shifted = jax.random.randint(jax.random.fold_in(key, 1), (pairs,), 0, 1 << 20) % (slack + 1)
    lengths = lengths.at[1:1 + 2 * pairs:2].set(donor - shifted).at[2:2 + 2 * pairs:2].set(sink + shifted)
    return lengths[jax.random.permutation(jax.random.fold_in(key, 2), count)]


def centred(stream_key, extent, deviation, reach, kind=jnp.bfloat16):
    return jnp.clip(deviation * jax.random.normal(stream_key, extent, jnp.float32), -reach, reach).astype(kind)


def setup_inputs(seed: int = 0) -> dict:
    streams_of = jax.random.split(jax.random.key(seed), 11)
    return {
        "pair_rep": draw_pair_rep(jax.random.fold_in(streams_of[10], 71), 0),
        "chain_id": jnp.searchsorted(jnp.cumsum(uneven_parts(streams_of[1], CHAINS, NRES, NRES // 2, 0)), jnp.arange(NRES), side="right").astype(jnp.int32),
        "live_mask": draw_live_mask(jax.random.fold_in(streams_of[10], 71), 0),
        "chain_table": centred(streams_of[3], (2, CZ), 1.0, 4.0, jnp.float32),
        "tri_proj": centred(streams_of[4], (2, CZ, 4 * CH), CZ ** -0.5, 0.5),
        "tri_gate": centred(streams_of[5], (2, CZ, CZ), CZ ** -0.5, 0.5),
        "tri_out": centred(streams_of[6], (2, CH, CZ), CH ** -0.5, 0.5),
        "att_project": centred(streams_of[7], (2, CZ, 4 * CZ), CZ ** -0.5, 0.5),
        "att_bias": draw_att_bias(jax.random.fold_in(streams_of[10], 71), 0),
        "att_out": centred(streams_of[9], (2, CZ, CZ), CZ ** -0.5, 0.5),
    }


def layer_norm(values):
    center = values - lax.optimization_barrier(jnp.mean(values, axis=-1, keepdims=True))
    spread = lax.optimization_barrier(jnp.mean(center * center, axis=-1, keepdims=True))
    return center / jnp.sqrt(spread + 1e-05)

def triangle_update(pair_state, pair_mask, weights, gate_weight, out_weight, incoming):
    normed = layer_norm(pair_state).astype(jnp.bfloat16)
    flat_in = normed.reshape(NRES * NRES, CZ)
    projected = jnp.dot(flat_in, weights, preferred_element_type=jnp.float32).reshape(NRES, NRES, 4 * CH)
    masked = pair_mask[:, :, None]
    left_side = (masked * jax.nn.sigmoid(projected[:, :, CH:2 * CH]) * projected[:, :, :CH]).astype(jnp.bfloat16)
    right_side = (masked * jax.nn.sigmoid(projected[:, :, 3 * CH:]) * projected[:, :, 2 * CH:3 * CH]).astype(jnp.bfloat16)
    left_side = lax.optimization_barrier(left_side)
    right_side = lax.optimization_barrier(right_side)
    left_wide = left_side.astype(jnp.float32)
    right_wide = right_side.astype(jnp.float32)
    if incoming:
        product = jnp.einsum('kic,kjc->ijc', left_wide, right_wide, precision=lax.Precision.HIGHEST)
    else:
        product = jnp.einsum('ikc,jkc->ijc', left_wide, right_wide, precision=lax.Precision.HIGHEST)
    mixed_norm = layer_norm(product).astype(jnp.bfloat16)
    gate_value = jax.nn.sigmoid(jnp.dot(flat_in, gate_weight, preferred_element_type=jnp.float32))
    update = gate_value * jnp.dot(mixed_norm.reshape(NRES * NRES, CH), out_weight, preferred_element_type=jnp.float32)
    return pair_state + update.reshape(NRES, NRES, CZ)

def line_attention(line_rows, pair_bias, key_bias, weights, out_weight):
    projected = jnp.dot(line_rows.reshape(NRES * NRES, CZ), weights, preferred_element_type=jnp.float32)
    projected = projected.reshape(NRES, NRES, 4, HEADS, DH)
    rounded = lax.optimization_barrier(projected[:, :, :3].astype(jnp.bfloat16))
    query = rounded[:, :, 0].astype(jnp.float32)
    keys = rounded[:, :, 1].astype(jnp.float32)
    values = rounded[:, :, 2].astype(jnp.float32)
    gate_value = jax.nn.sigmoid(projected[:, :, 3])
    scaling = DH ** (-0.5)

    def one_block(offset):
        query_block = lax.dynamic_slice_in_dim(query, offset, RES_COL, 0)
        keys_block = lax.dynamic_slice_in_dim(keys, offset, RES_COL, 0)
        values_block = lax.dynamic_slice_in_dim(values, offset, RES_COL, 0)
        scores = jnp.einsum('ijhd,ikhd->hijk', query_block, keys_block, precision=lax.Precision.HIGHEST) * scaling + pair_bias[:, None] + key_bias
        scores = scores - lax.optimization_barrier(jnp.max(scores, axis=-1, keepdims=True))
        exponent = jnp.exp(scores)
        weight = (exponent / lax.optimization_barrier(jnp.sum(exponent, axis=-1, keepdims=True))).astype(jnp.bfloat16)
        weight = lax.optimization_barrier(weight).astype(jnp.float32)
        return jnp.einsum('hijk,ikhd->ijhd', weight, values_block, precision=lax.Precision.HIGHEST)
    starts = jnp.arange(NRES // RES_COL, dtype=jnp.int32) * RES_COL
    attended = lax.map(one_block, starts).reshape(NRES, NRES, HEADS, DH)
    gated = (gate_value * attended).astype(jnp.bfloat16).reshape(NRES * NRES, CZ)
    update = jnp.dot(gated, out_weight, preferred_element_type=jnp.float32).astype(jnp.bfloat16)
    return update.reshape(NRES, NRES, CZ)

def attention_update(pair_state, key_bias, weights, bias_weight, out_weight, column):
    normed = layer_norm(pair_state)
    lowered = normed.astype(jnp.bfloat16)
    pair_bias = jnp.einsum('abc,ch->hab', normed, bias_weight, precision=lax.Precision.HIGHEST)
    if column:
        lowered = jnp.swapaxes(lowered, 0, 1)
        pair_bias = jnp.swapaxes(pair_bias, 1, 2)
    update = line_attention(lowered, pair_bias, key_bias, weights, out_weight)
    if column:
        update = jnp.swapaxes(update, 0, 1)
    return pair_state + update.astype(jnp.float32)

def reference(pair_rep, chain_id, live_mask, chain_table, tri_proj, tri_gate, tri_out, att_project, att_bias, att_out):
    same_chain = chain_id[:, None] == chain_id[None, :]
    pair_state = pair_rep + jnp.where(same_chain[:, :, None], chain_table[1], chain_table[0])
    live_float = live_mask.astype(jnp.float32)
    pair_mask = live_float[:, None] * live_float[None, :]
    key_bias = (live_float - 1.0) * 1000000000.0
    pair_state = triangle_update(pair_state, pair_mask, tri_proj[0], tri_gate[0], tri_out[0], False)
    pair_state = triangle_update(pair_state, pair_mask, tri_proj[1], tri_gate[1], tri_out[1], True)
    pair_state = attention_update(pair_state, key_bias, att_project[0], att_bias[0], att_out[0], False)
    pair_state = attention_update(pair_state, key_bias, att_project[1], att_bias[1], att_out[1], True)
    return pair_state
```

```python
import functools
import jax
import jax.numpy as jnp
from jax import lax
from jax.sharding import PartitionSpec as P
from jax.experimental import pallas as pl
from jax.experimental.pallas import tpu as pltpu

F32 = jnp.float32
BF16 = jnp.bfloat16
MESH = pl.DeviceIdType.MESH
CZ = 128
ROWS, COLS = 8, 16
IL, JL = 48, 24
PX = IL * JL
NRES = 384
NDEV = ROWS * COLS
QS = PX // 128
GO, BACK = 32, 16
GO32, BACK32 = 24, 16


def normalize(v):
    mean = jnp.mean(v, axis=-1, keepdims=True)
    c = v - mean
    spread = jnp.mean(c * c, axis=-1, keepdims=True)
    return c * lax.rsqrt(spread + 1e-05)


def dot(a, b, dims=((1,), (0,))):
    return lax.dot_general(a, b, (dims, ((), ())), preferred_element_type=F32)


def exchange_start(src, dst, send, recv, r, s):
    me = r * COLS + s

    def go(d, _):
        p = jnp.bitwise_xor(me, d)
        pltpu.make_async_remote_copy(
            src_ref=src.at[p], dst_ref=dst.at[me], send_sem=send, recv_sem=recv,
            device_id=(p // COLS, p % COLS), device_id_type=MESH,
        ).start()
        return 0

    lax.fori_loop(1, NDEV, go, 0)
    dst[me] = src[me]


def exchange_wait(src, dst, send, recv):
    part = pl.ds(0, NDEV - 1)
    pltpu.make_async_copy(src.at[part], dst.at[part], recv).wait()
    pltpu.make_async_copy(src.at[part], dst.at[part], send).wait()


def triangle(t, x, mask, proj, gate, out, nb, stage, send_go, recv_go, send_back, recv_back, left, right, sems, r, s, before_send):
    def side(q, _):
        rows = pl.ds(pl.multiple_of(q * 128, 128), 128)
        n = normalize(x[rows, :]).astype(BF16)
        nb[rows, :] = n
        p = dot(n, proj[t])
        m = mask[pl.ds(q, 1), :]
        for k in range(2):
            v = jax.nn.sigmoid(p[:, (2 * k + 1) * CZ:(2 * k + 2) * CZ]) * p[:, 2 * k * CZ:(2 * k + 1) * CZ]
            stage[pl.ds(k * QS + q, CZ, stride=GO32), :] = v.T * m
        return 0

    lax.fori_loop(0, QS, side, 0)

    def pack(c, _):
        f = stage[pl.ds(pl.multiple_of(c * GO32, GO32), GO32), :]
        send_go[c] = jnp.concatenate([f, jnp.zeros((GO - GO32, 128), F32)], axis=0).astype(BF16)
        return 0

    lax.fori_loop(0, CZ, pack, 0, unroll=4)
    before_send()
    exchange_start(send_go, recv_go, sems.at[0], sems.at[1], r, s)
    exchange_wait(send_go, recv_go, sems.at[0], sems.at[1])

    def unpack(c, _):
        stage[pl.ds(pl.multiple_of(c * GO32, GO32), GO32), :] = recv_go[c].astype(F32)[:GO32]
        return 0

    lax.fori_loop(0, NDEV, unpack, 0, unroll=4)

    for k, ref in enumerate((left, right)):
        def gather(a, _):
            v = []
            for rr in range(ROWS):
                v.append(jnp.concatenate(
                    [stage[pl.ds(rr * COLS * GO32 + k * QS + 3 * a + i, COLS, stride=GO32), :] for i in range(3)], axis=1))
            for b in range(8):
                row = jnp.concatenate([u[:, IL * b:IL * (b + 1)] for u in v], axis=1)
                for i in range(3):
                    ref[pl.ds(i * NRES + 8 * a + b, COLS, stride=JL), :] = row[:, 128 * i:128 * (i + 1)]
            return 0

        lax.fori_loop(0, 3, gather, 0)
    lf = jnp.concatenate([left[pl.ds(i * NRES, NRES), :] for i in range(3)], axis=1).astype(BF16)
    rt = jnp.concatenate([right[pl.ds(i * NRES, NRES), :] for i in range(3)], axis=1).astype(BF16)
    prod = dot(rt, lf, ((0,), (0,))) if t == 0 else dot(rt, lf, ((1,), (1,)))
    for i in range(3):
        left[pl.ds(i * NRES, NRES), :] = prod[:, 128 * i:128 * (i + 1)]

    def scatter(a, _):
        v = []
        for b in range(8):
            v.append(jnp.concatenate([left[pl.ds(i * NRES + 8 * a + b, COLS, stride=JL), :] for i in range(3)], axis=1))
        for rr in range(ROWS):
            row = jnp.concatenate([u[:, IL * rr:IL * (rr + 1)] for u in v], axis=1)
            for i in range(3):
                stage[pl.ds(rr * COLS * BACK32 + 3 * a + i, COLS, stride=BACK32), :] = row[:, 128 * i:128 * (i + 1)]
        return 0

    lax.fori_loop(0, 3, scatter, 0)

    def pack2(c, _):
        send_back[c] = stage[pl.ds(pl.multiple_of(c * BACK32, BACK32), BACK32), :].astype(BF16)
        return 0

    lax.fori_loop(0, NDEV, pack2, 0, unroll=4)
    exchange_start(send_back, recv_back, sems.at[2], sems.at[3], r, s)
    exchange_wait(send_back, recv_back, sems.at[2], sems.at[3])

    def unpack2(c, _):
        stage[pl.ds(pl.multiple_of(c * BACK32, BACK32), BACK32), :] = recv_back[c].astype(F32)
        return 0

    lax.fori_loop(0, CZ, unpack2, 0, unroll=4)

    def finish(q, _):
        rows = pl.ds(pl.multiple_of(q * 128, 128), 128)
        pr = stage[pl.ds(q, CZ, stride=BACK32), :].T
        mixed = normalize(pr).astype(BF16)
        g = jax.nn.sigmoid(dot(nb[rows, :], gate[t]))
        x[rows, :] = x[rows, :] + g * dot(mixed, out[t])
        return 0

    lax.fori_loop(0, QS, finish, 0)


def tri_kernel(pair, mask, same, table, proj, gate, out, y, x, nb, stage, sg0, rg0, sb0, rb0, sg1, rg1, sb1, rb1, left, right, sems):
    r = lax.axis_index("row")
    s = lax.axis_index("col")
    me = r * COLS + s
    barrier = pltpu.get_barrier_semaphore()

    def greet(d, _):
        p = jnp.bitwise_xor(me, d)
        pl.semaphore_signal(barrier, inc=1, device_id=(p // COLS, p % COLS), device_id_type=MESH)
        return 0

    lax.fori_loop(1, NDEV, greet, 0)
    stage[...] = jnp.zeros_like(stage)
    for j in range(JL):
        part = pl.ds(j * IL, IL)
        x[part, :] = pair[pl.ds(j, IL, stride=JL), :] + jnp.where(same[part, :] > 0, table[1:2, :], table[0:1, :])
    triangle(0, x, mask, proj, gate, out, nb, stage, sg0, rg0, sb0, rb0, left, right, sems.at[0], r, s,
             lambda: pl.semaphore_wait(barrier, NDEV - 1))
    triangle(1, x, mask, proj, gate, out, nb, stage, sg1, rg1, sb1, rb1, left, right, sems.at[1], r, s, lambda: None)
    for j in range(JL):
        y[pl.ds(j, IL, stride=JL), :] = x[pl.ds(j * IL, IL), :]


def tri_call(pair, mask, same, table, proj, gate, out):
    vm = pl.BlockSpec(memory_space=pltpu.VMEM)
    bufs = []
    for _ in range(2):
        bufs += [pltpu.VMEM((NDEV, GO, 128), BF16)] * 2 + [pltpu.VMEM((NDEV, BACK, 128), BF16)] * 2
    return pl.pallas_call(
        tri_kernel,
        out_shape=jax.ShapeDtypeStruct((PX, CZ), F32),
        in_specs=[vm] * 7,
        out_specs=vm,
        scratch_shapes=[
            pltpu.VMEM((PX, CZ), F32),
            pltpu.VMEM((PX, CZ), BF16),
            pltpu.VMEM((NDEV * GO32, 128), F32),
            *bufs,
            pltpu.VMEM((3 * NRES, 128), F32),
            pltpu.VMEM((3 * NRES, 128), F32),
            pltpu.SemaphoreType.DMA((2, 4)),
        ],
        compiler_params=pltpu.CompilerParams(collective_id=0, has_side_effects=True, vmem_limit_bytes=48 << 20),
    )(pair, mask, same, table, proj, gate, out)


HEADS = 4
DH = 32


def layer_norm(values):
    center = values - jnp.mean(values, axis=-1, keepdims=True)
    spread = jnp.mean(center * center, axis=-1, keepdims=True)
    return center / jnp.sqrt(spread + 1e-05)


def full_bias(normed, bias_weight, row_count, col_count):
    rows_here, cols_here = (normed.shape[0], normed.shape[1])
    tile_bias = jnp.dot(
        normed.reshape(rows_here * cols_here, CZ),
        bias_weight,
        precision=lax.Precision.HIGHEST,
        preferred_element_type=jnp.float32,
    )
    tile_bias = jnp.transpose(tile_bias.reshape(rows_here, cols_here, HEADS), (2, 0, 1))
    gathered = lax.all_gather(tile_bias, ("row", "col"), axis=0, tiled=True)
    gathered = gathered.reshape(row_count, col_count, HEADS, rows_here, cols_here)
    gathered = jnp.transpose(gathered, (2, 0, 3, 1, 4))
    return gathered.reshape(HEADS, row_count * rows_here, col_count * cols_here)


def attend_heads(query_all, keys_all, values_all, pair_bias, key_bias, flipped):
    scaling = DH ** (-0.5)

    def one_head(inputs):
        query_head, keys_head, values_head, bias_head = inputs
        if flipped:
            bias_head = bias_head.T
        scores = (
            jnp.einsum("ijd,ikd->ijk", query_head, keys_head, preferred_element_type=jnp.float32)
            * scaling
            + bias_head[None]
            + key_bias
        )
        scores = scores - jnp.max(scores, axis=-1, keepdims=True)
        exponent = jnp.exp(scores)
        weight = (exponent / jnp.sum(exponent, axis=-1, keepdims=True)).astype(jnp.bfloat16)
        return jnp.einsum("ijk,ikd->ijd", weight, values_head, preferred_element_type=jnp.float32)

    return lax.map(one_head, (query_all, keys_all, values_all, pair_bias))


def line_update(line_rows, pair_bias, key_bias, weights, out_weight, flipped):
    first_dim, second_dim = (line_rows.shape[0], line_rows.shape[1])
    projected = jnp.dot(
        line_rows.reshape(first_dim * second_dim, CZ), weights, preferred_element_type=jnp.float32
    )
    projected = projected.reshape(first_dim, second_dim, 4, HEADS, DH)
    rounded = projected[:, :, :3].astype(jnp.bfloat16)
    axes_order = (2, 3, 1, 0, 4) if flipped else (2, 3, 0, 1, 4)
    heads_first = jnp.transpose(rounded, axes_order)
    attended = attend_heads(
        heads_first[0], heads_first[1], heads_first[2], pair_bias, key_bias, flipped
    )
    back_order = (2, 1, 0, 3) if flipped else (1, 2, 0, 3)
    attended = jnp.transpose(attended, back_order)
    gate_value = jax.nn.sigmoid(projected[:, :, 3])
    gated = (gate_value * attended).astype(jnp.bfloat16).reshape(first_dim * second_dim, CZ)
    update = jnp.dot(gated, out_weight, preferred_element_type=jnp.float32).astype(jnp.bfloat16)
    return update.reshape(first_dim, second_dim, CZ)


def local(
    pair_rep,
    chain_id,
    live_mask,
    chain_table,
    tri_proj,
    tri_gate,
    tri_out,
    att_project,
    att_bias,
    att_out,
):
    rows_here, cols_here = (pair_rep.shape[0], pair_rep.shape[1])
    row_count = lax.axis_size("row")
    col_count = lax.axis_size("col")
    row_index = lax.axis_index("row")
    col_index = lax.axis_index("col")
    chain_rows = lax.dynamic_slice_in_dim(chain_id, row_index * rows_here, rows_here)
    chain_cols = lax.dynamic_slice_in_dim(chain_id, col_index * cols_here, cols_here)
    live_float = live_mask.astype(jnp.float32)
    live_rows = lax.dynamic_slice_in_dim(live_float, row_index * rows_here, rows_here)
    live_cols = lax.dynamic_slice_in_dim(live_float, col_index * cols_here, cols_here)
    same_chain = chain_rows[:, None] == chain_cols[None, :]
    mask = (live_cols[:, None] * live_rows[None, :]).reshape(QS, 128)
    same = jnp.broadcast_to(same_chain.T.reshape(PX, 1), (PX, CZ)).astype(jnp.int32)
    key_bias = (live_float - 1.0) * 1000000000.0
    pair_state = tri_call(
        pair_rep.reshape(PX, CZ), mask, same, chain_table, tri_proj, tri_gate, tri_out
    ).reshape(rows_here, cols_here, CZ)
    normed = layer_norm(pair_state)
    pair_bias = full_bias(normed, att_bias[0], row_count, col_count)
    line_rows = lax.all_to_all(
        normed.astype(jnp.bfloat16), "col", split_axis=0, concat_axis=1, tiled=True
    )
    update = line_update(line_rows, pair_bias, key_bias, att_project[0], att_out[0], False)
    returned = lax.all_to_all(update, "col", split_axis=1, concat_axis=0, tiled=True)
    pair_state = pair_state + returned.astype(jnp.float32)
    normed = layer_norm(pair_state)
    pair_bias = full_bias(normed, att_bias[1], row_count, col_count)
    line_cols = lax.all_to_all(
        normed.astype(jnp.bfloat16), "row", split_axis=1, concat_axis=0, tiled=True
    )
    update = line_update(line_cols, pair_bias, key_bias, att_project[1], att_out[1], True)
    returned = lax.all_to_all(update, "row", split_axis=0, concat_axis=1, tiled=True)
    pair_state = pair_state + returned.astype(jnp.float32)
    return pair_state


def solution(mesh):
    return jax.shard_map(
        local,
        mesh=mesh,
        in_specs=(P("row", "col", None), P(), P(), P(), P(), P(), P(), P(), P(), P()),
        out_specs=P("row", "col", None),
        check_vma=False,
    )
```

```python
import jax
import jax.numpy as jnp
from jax import lax
from jax.sharding import PartitionSpec as P
from jax.experimental import pallas as pl
from jax.experimental.pallas import tpu as pltpu

F32 = jnp.float32
BF16 = jnp.bfloat16
MESH = pl.DeviceIdType.MESH
CZ = 128
ROWS, COLS = 8, 16
IL, JL = 48, 24
PX = IL * JL
NRES = 384
NDEV = ROWS * COLS
QS = PX // 128
HEADS, DH = 4, 32
STRIP = HEADS * 3 * JL
LINE0 = 80
LOG2E = 1.4426950408889634
SCALE = DH ** -0.5
GO, BACK = 32, 16
GO32, BACK32 = 24, 16


def normalize(v):
    mean = jnp.mean(v, axis=-1, keepdims=True)
    c = v - mean
    spread = jnp.mean(c * c, axis=-1, keepdims=True)
    return c * lax.rsqrt(spread + 1e-05)


def dot(a, b, dims=((1,), (0,))):
    return lax.dot_general(a, b, (dims, ((), ())), preferred_element_type=F32)


def exchange_start(src, dst, send, recv, r, s):
    me = r * COLS + s

    def go(d, _):
        p = jnp.bitwise_xor(me, d)
        pltpu.make_async_remote_copy(
            src_ref=src.at[p], dst_ref=dst.at[me], send_sem=send, recv_sem=recv,
            device_id=(p // COLS, p % COLS), device_id_type=MESH,
        ).start()
        return 0

    lax.fori_loop(1, NDEV, go, 0)
    dst[me] = src[me]


def exchange_wait(src, dst, send, recv):
    part = pl.ds(0, NDEV - 1)
    pltpu.make_async_copy(src.at[part], dst.at[part], recv).wait()
    pltpu.make_async_copy(src.at[part], dst.at[part], send).wait()


def triangle(t, x, mask, proj, gate, out, nb, stage, send_go, recv_go, send_back, recv_back, left, right, sems, r, s, before_send):
    def side(q, _):
        rows = pl.ds(pl.multiple_of(q * 128, 128), 128)
        n = normalize(x[rows, :]).astype(BF16)
        nb[rows, :] = n
        p = dot(n, proj[t])
        m = mask[pl.ds(q, 1), :]
        for k in range(2):
            v = jax.nn.sigmoid(p[:, (2 * k + 1) * CZ:(2 * k + 2) * CZ]) * p[:, 2 * k * CZ:(2 * k + 1) * CZ]
            stage[pl.ds(k * QS + q, CZ, stride=GO32), :] = v.T * m
        return 0

    lax.fori_loop(0, QS, side, 0)

    def pack(c, _):
        f = stage[pl.ds(pl.multiple_of(c * GO32, GO32), GO32), :]
        send_go[c] = jnp.concatenate([f, jnp.zeros((GO - GO32, 128), F32)], axis=0).astype(BF16)
        return 0

    lax.fori_loop(0, CZ, pack, 0, unroll=4)
    before_send()
    exchange_start(send_go, recv_go, sems.at[0], sems.at[1], r, s)
    exchange_wait(send_go, recv_go, sems.at[0], sems.at[1])

    def unpack(c, _):
        stage[pl.ds(pl.multiple_of(c * GO32, GO32), GO32), :] = recv_go[c].astype(F32)[:GO32]
        return 0

    lax.fori_loop(0, NDEV, unpack, 0, unroll=4)

    for k, ref in enumerate((left, right)):
        def gather(a, _):
            v = []
            for rr in range(ROWS):
                v.append(jnp.concatenate(
                    [stage[pl.ds(rr * COLS * GO32 + k * QS + 3 * a + i, COLS, stride=GO32), :] for i in range(3)], axis=1))
            for b in range(8):
                row = jnp.concatenate([u[:, IL * b:IL * (b + 1)] for u in v], axis=1)
                for i in range(3):
                    ref[pl.ds(i * NRES + 8 * a + b, COLS, stride=JL), :] = row[:, 128 * i:128 * (i + 1)]
            return 0

        lax.fori_loop(0, 3, gather, 0)
    lf = jnp.concatenate([left[pl.ds(i * NRES, NRES), :] for i in range(3)], axis=1).astype(BF16)
    rt = jnp.concatenate([right[pl.ds(i * NRES, NRES), :] for i in range(3)], axis=1).astype(BF16)
    prod = dot(rt, lf, ((0,), (0,))) if t == 0 else dot(rt, lf, ((1,), (1,)))
    for i in range(3):
        left[pl.ds(i * NRES, NRES), :] = prod[:, 128 * i:128 * (i + 1)]

    def scatter(a, _):
        v = []
        for b in range(8):
            v.append(jnp.concatenate([left[pl.ds(i * NRES + 8 * a + b, COLS, stride=JL), :] for i in range(3)], axis=1))
        for rr in range(ROWS):
            row = jnp.concatenate([u[:, IL * rr:IL * (rr + 1)] for u in v], axis=1)
            for i in range(3):
                stage[pl.ds(rr * COLS * BACK32 + 3 * a + i, COLS, stride=BACK32), :] = row[:, 128 * i:128 * (i + 1)]
        return 0

    lax.fori_loop(0, 3, scatter, 0)

    def pack2(c, _):
        send_back[c] = stage[pl.ds(pl.multiple_of(c * BACK32, BACK32), BACK32), :].astype(BF16)
        return 0

    lax.fori_loop(0, NDEV, pack2, 0, unroll=4)
    exchange_start(send_back, recv_back, sems.at[2], sems.at[3], r, s)
    exchange_wait(send_back, recv_back, sems.at[2], sems.at[3])

    def unpack2(c, _):
        stage[pl.ds(pl.multiple_of(c * BACK32, BACK32), BACK32), :] = recv_back[c].astype(F32)
        return 0

    lax.fori_loop(0, CZ, unpack2, 0, unroll=4)

    def finish(q, _):
        rows = pl.ds(pl.multiple_of(q * 128, 128), 128)
        pr = stage[pl.ds(q, CZ, stride=BACK32), :].T
        mixed = normalize(pr).astype(BF16)
        g = jax.nn.sigmoid(dot(nb[rows, :], gate[t]))
        x[rows, :] = x[rows, :] + g * dot(mixed, out[t])
        return 0

    lax.fori_loop(0, QS, finish, 0)

def group_start(axis, src, dst, send, recv, r, s):
    n, me = (ROWS, r) if axis == "row" else (COLS, s)

    def go(d, _):
        p = jnp.bitwise_xor(me, d)
        pltpu.make_async_remote_copy(
            src_ref=src(p), dst_ref=dst(me), send_sem=send, recv_sem=recv,
            device_id=(p, s) if axis == "row" else (r, p), device_id_type=MESH,
        ).start()
        return 0

    lax.fori_loop(1, n, go, 0)


def drain(ref, count, sem):
    part = ref.at[pl.ds(0, count)]
    pltpu.make_async_copy(part, part, sem).wait()


def strip(ref, slot):
    return ref.at[pl.ds(pl.multiple_of(slot * STRIP, 8), STRIP)]


def attention(t, x, kb, bias_w, w_project, w_out, nf, p1, bias, msg, got, upd, back, line, qs, ks, vs, gs, vt, us, sems, slots, r, s):
    axis, peers, per = ("col", COLS, LINE0) if t == 0 else ("row", ROWS, 3 * IL)
    xl, rest = s // 8, s % 8
    yy, core = rest // 2, rest % 2

    def at(dx, dy, dc):
        return ((xl + dx) % 2) * 8 + ((yy + dy) % 4) * 2 + (core + dc) % 2

    def chunk(q, _):
        rows = pl.ds(pl.multiple_of(q * 128, 128), 128)
        n = normalize(x[rows, :])
        nf[rows, :] = n
        b8 = lax.dot_general(bias_w[t], n, (((1,), (1,)), ((), ())), precision=lax.Precision.HIGHEST, preferred_element_type=F32)
        p1[r, q] = (b8[:HEADS] + kb[t, pl.ds(q, 1), :]) * LOG2E
        return 0

    lax.fori_loop(0, QS, chunk, 0)
    group_start("row", lambda p: p1.at[r], lambda m: p1.at[m], sems.at[0], sems.at[1], r, s)

    if t == 0:
        for p in range(COLS):
            v = [nf[pl.ds(3 * p + u, JL, stride=IL), :] for u in range(3)]
            msg[p] = jnp.concatenate(v + [jnp.zeros((LINE0 - 72, CZ), F32)], axis=0).astype(BF16)
    else:
        for p in range(ROWS):
            msg[p] = nf[pl.ds(p * per, per), :].astype(BF16)
    group_start(axis, lambda p: msg.at[p], lambda m: got.at[m], sems.at[2], sems.at[3], r, s)
    me = s if t == 0 else r
    got[me] = msg[me]

    drain(p1, ROWS - 1, sems.at[1])

    def lay(a, _):
        v = [jnp.concatenate([p1[rr, 3 * a + i] for i in range(3)], axis=1) for rr in range(ROWS)]
        for b in range(8):
            row = jnp.concatenate([u[:, IL * b:IL * (b + 1)] for u in v], axis=1)
            for i in range(3):
                bias[pl.ds(s * STRIP + i * JL + 8 * a + b, HEADS, stride=3 * JL), :] = row[:, 128 * i:128 * (i + 1)]
        return 0

    lax.fori_loop(0, 3, lay, 0)

    def pass_on(slot, target):
        pltpu.make_async_remote_copy(
            src_ref=strip(bias, slot), dst_ref=strip(bias, slot), send_sem=sems.at[4], recv_sem=slots.at[slot],
            device_id=(r, target), device_id_type=MESH,
        ).start()

    def arrived(slot):
        pltpu.make_async_copy(strip(bias, slot), strip(bias, slot), slots.at[slot]).wait()

    for d in ((1, 0, 0), (0, 1, 0), (0, 3, 0), (0, 2, 0), (0, 0, 1)):
        pass_on(s, at(*d))

    drain(got, peers - 1, sems.at[3])
    if t == 0:
        for p in range(COLS):
            v = got[p].astype(F32)
            for u in range(3):
                line[pl.ds(u * NRES + p * JL, JL), :] = v[u * JL:(u + 1) * JL]
    else:
        for p in range(ROWS):
            for u in range(3):
                line[pl.ds(u * NRES + p * IL, IL), :] = got[p, u * IL:(u + 1) * IL, :].astype(F32)

    def project(u):
        rows = pl.ds(u * NRES, NRES)
        p = dot(line[rows, :].astype(BF16), w_project[t])
        qs[rows, :] = p[:, :CZ].astype(BF16)
        ks[rows, :] = p[:, CZ:2 * CZ].astype(BF16)
        v = p[:, 2 * CZ:3 * CZ]
        if t == 0:
            vt[pl.ds(u * CZ, CZ), :] = v.T.astype(BF16)
        else:
            vs[rows, :] = v.astype(BF16)
        gs[rows, :] = jax.nn.sigmoid(p[:, 3 * CZ:])

    project(0)
    arrived(at(1, 0, 0))
    for d in ((0, 1, 0), (0, 3, 0), (0, 0, 1)):
        pass_on(at(1, 0, 0), at(*d))
    arrived(at(0, 2, 0))
    for d in ((1, 0, 0), (0, 0, 1)):
        pass_on(at(0, 2, 0), at(*d))
    project(1)
    for d in ((0, 1, 0), (0, 3, 0), (1, 1, 0), (1, 3, 0), (1, 2, 0)):
        arrived(at(*d))
        pass_on(at(*d), at(0, 0, 1))
    project(2)
    for dx in range(2):
        for dy in range(4):
            arrived(at(dx, dy, 1))

    lane_head = lax.broadcasted_iota(jnp.int32, (1, CZ), 1) // DH

    def scores_max(e):
        return jnp.exp2(e - jnp.max(e, axis=0 if t == 0 else 1, keepdims=True))

    if t == 0:
        def tile(n, _):
            u, i = n // 3, n % 3
            qrow = pl.ds(pl.multiple_of(n * 128, 128), 128)
            q = qs[qrow, :]
            k = ks[pl.ds(pl.multiple_of(u * NRES, 128), NRES), :]
            parts = []
            for h in range(HEADS):
                qh = jnp.where(lane_head == h, q, jnp.zeros_like(q))
                b = jnp.concatenate([bias[pl.ds(pl.multiple_of(p * STRIP + h * 3 * JL + i * JL, 8), JL), :] for p in range(COLS)], axis=0)
                e = scores_max(dot(k, qh, ((1,), (1,))) * (SCALE * LOG2E) + b)
                total = jnp.sum(e, axis=0, keepdims=True)
                o = dot(vt[pl.ds(pl.multiple_of(u * CZ + h * DH, DH), DH), :], e.astype(BF16))
                parts.append(o / total)
            att = jnp.concatenate(parts, axis=0).T
            gated = (gs[qrow, :] * att).astype(BF16)
            us[qrow, :] = dot(gated, w_out[t])
            return 0

        lax.fori_loop(0, 9, tile, 0)
        for p in range(COLS):
            v = [us[pl.ds(u * NRES + p * JL, JL), :] for u in range(3)]
            upd[p] = jnp.concatenate(v + [jnp.zeros((LINE0 - 72, CZ), F32)], axis=0).astype(BF16)
    else:
        def tile(n, _):
            u, i = n // 4, n % 4
            qrow = pl.ds(pl.multiple_of(n * 96, 32), 96)
            lrow = pl.ds(pl.multiple_of(u * NRES, 128), NRES)
            q, k, v = qs[qrow, :], ks[lrow, :], vs[lrow, :]
            att = jnp.zeros((96, CZ), F32)
            for h in range(HEADS):
                kh = jnp.where(lane_head == h, k, jnp.zeros_like(k))
                vh = jnp.concatenate([jnp.where(lane_head == h, v, jnp.zeros_like(v)), jnp.ones_like(v)], axis=1)
                b = jnp.concatenate([
                    jnp.concatenate([bias[pl.ds(pl.multiple_of((4 * i + p) * STRIP + h * 3 * JL + w * JL, 8), JL), :] for p in range(4)], axis=0)
                    for w in range(3)], axis=1)
                e = scores_max(dot(q, kh, ((1,), (1,))) * (SCALE * LOG2E) + b)
                o = dot(e.astype(BF16), vh)
                att = att + o[:, :CZ] / o[:, CZ:]
            gated = (gs[qrow, :] * att).astype(BF16)
            us[qrow, :] = dot(gated, w_out[t])
            return 0

        lax.fori_loop(0, 12, tile, 0)
        for p in range(ROWS):
            for u in range(3):
                upd[p, u * IL:(u + 1) * IL, :] = us[pl.ds(u * NRES + p * IL, IL), :].astype(BF16)

    group_start(axis, lambda p: upd.at[p], lambda m: back.at[m], sems.at[5], sems.at[6], r, s)
    back[me] = upd[me]
    drain(back, peers - 1, sems.at[6])
    if t == 0:
        for p in range(COLS):
            v = back[p].astype(F32)
            for u in range(3):
                rows = pl.ds(3 * p + u, JL, stride=IL)
                x[rows, :] = x[rows, :] + v[u * JL:(u + 1) * JL]
    else:
        for p in range(ROWS):
            rows = pl.ds(p * per, per)
            x[rows, :] = x[rows, :] + back[p].astype(F32)
    drain(p1, ROWS - 1, sems.at[0])
    drain(msg, peers - 1, sems.at[2])
    pltpu.make_async_copy(bias.at[pl.ds(0, 15 * STRIP)], bias.at[pl.ds(0, 15 * STRIP)], sems.at[4]).wait()
    drain(upd, peers - 1, sems.at[5])


def kernel(pair, mask, kb, same, table, proj, gate, out, att_w, bias_w, att_o, y, x, nb, stage,
           sg0, rg0, sb0, rb0, sg1, rg1, sb1, rb1, left, right, *more):
    att0, att1, shared, sems, asems, slots = more[:6], more[6:12], more[12:20], more[20], more[21], more[22]
    r = lax.axis_index("row")
    s = lax.axis_index("col")
    me = r * COLS + s
    barrier = pltpu.get_barrier_semaphore()

    def greet(d, _):
        p = jnp.bitwise_xor(me, d)
        pl.semaphore_signal(barrier, inc=1, device_id=(p // COLS, p % COLS), device_id_type=MESH)
        return 0

    lax.fori_loop(1, NDEV, greet, 0)
    stage[...] = jnp.zeros_like(stage)
    for j in range(JL):
        part = pl.ds(j * IL, IL)
        x[part, :] = pair[pl.ds(j, IL, stride=JL), :] + jnp.where(same[part, :] > 0, table[1:2, :], table[0:1, :])
    triangle(0, x, mask, proj, gate, out, nb, stage, sg0, rg0, sb0, rb0, left, right, sems.at[0], r, s,
             lambda: pl.semaphore_wait(barrier, NDEV - 1))
    triangle(1, x, mask, proj, gate, out, nb, stage, sg1, rg1, sb1, rb1, left, right, sems.at[1], r, s, lambda: None)
    for t, bufs in ((0, att0), (1, att1)):
        nf, line, qs, ks, vs, gs, vt, us = shared
        attention(t, x, kb, bias_w, att_w, att_o, nf, *bufs, line, qs, ks, vs, gs, vt, us, asems.at[t], slots.at[t], r, s)
    for j in range(JL):
        y[pl.ds(j, IL, stride=JL), :] = x[pl.ds(j * IL, IL), :]


def call(*args):
    vm = pl.BlockSpec(memory_space=pltpu.VMEM)
    bufs = []
    for _ in range(2):
        bufs += [pltpu.VMEM((NDEV, GO, 128), BF16)] * 2 + [pltpu.VMEM((NDEV, BACK, 128), BF16)] * 2
    lines = [
        [pltpu.VMEM((ROWS, QS, HEADS, 128), F32), pltpu.VMEM((COLS * STRIP, 128), F32)]
        + [pltpu.VMEM(shape, BF16)] * 4
        for shape in ((COLS, LINE0, CZ), (ROWS, 3 * IL, CZ))
    ]
    tall = (3 * NRES, 128)
    return pl.pallas_call(
        kernel,
        out_shape=jax.ShapeDtypeStruct((PX, CZ), F32),
        in_specs=[vm] * len(args),
        out_specs=vm,
        scratch_shapes=[
            pltpu.VMEM((PX, CZ), F32),
            pltpu.VMEM((PX, CZ), BF16),
            pltpu.VMEM((NDEV * GO32, 128), F32),
            *bufs,
            pltpu.VMEM(tall, F32),
            pltpu.VMEM(tall, F32),
            *lines[0],
            *lines[1],
            pltpu.VMEM((PX, CZ), F32),
            pltpu.VMEM(tall, F32),
            pltpu.VMEM(tall, BF16),
            pltpu.VMEM(tall, BF16),
            pltpu.VMEM(tall, BF16),
            pltpu.VMEM(tall, F32),
            pltpu.VMEM((3 * CZ, NRES), BF16),
            pltpu.VMEM(tall, F32),
            pltpu.SemaphoreType.DMA((2, 4)),
            pltpu.SemaphoreType.DMA((2, 7)),
            pltpu.SemaphoreType.DMA((2, COLS)),
        ],
        compiler_params=pltpu.CompilerParams(collective_id=0, has_side_effects=True, vmem_limit_bytes=56 << 20),
    )(*args)


def local(pair_rep, chain_id, live_mask, chain_table, tri_proj, tri_gate, tri_out, att_project, att_bias, att_out):
    row_index = lax.axis_index("row")
    col_index = lax.axis_index("col")
    chain_rows = lax.dynamic_slice_in_dim(chain_id, row_index * IL, IL)
    chain_cols = lax.dynamic_slice_in_dim(chain_id, col_index * JL, JL)
    live = live_mask.astype(F32)
    live_rows = lax.dynamic_slice_in_dim(live, row_index * IL, IL)
    live_cols = lax.dynamic_slice_in_dim(live, col_index * JL, JL)
    mask = (live_cols[:, None] * live_rows[None, :]).reshape(QS, 128)
    zero = jnp.zeros((JL, IL), F32)
    key_bias = jnp.stack([zero + ((live_cols - 1.0) * 1e9)[:, None], zero + ((live_rows - 1.0) * 1e9)[None, :]]).reshape(2, QS, 128)
    same = (chain_cols[:, None] == chain_rows[None, :]).reshape(PX, 1)
    same = jnp.broadcast_to(same, (PX, CZ)).astype(jnp.int32)
    bias_w = jnp.pad(jnp.swapaxes(att_bias, 1, 2), ((0, 0), (0, 8 - HEADS), (0, 0)))
    pair_out = call(
        pair_rep.reshape(PX, CZ), mask, key_bias, same, chain_table, tri_proj, tri_gate, tri_out,
        att_project, bias_w, att_out,
    )
    return pair_out.reshape(pair_rep.shape)


def solution(mesh):
    return jax.shard_map(
        local,
        mesh=mesh,
        in_specs=(P("row", "col", None), P(), P(), P(), P(), P(), P(), P(), P(), P()),
        out_specs=P("row", "col", None),
        check_vma=False,
    )
```

```python
import jax
import jax.numpy as jnp
from jax import lax
from jax.sharding import PartitionSpec as P
from jax.experimental import pallas as pl
from jax.experimental.pallas import tpu as pltpu

F32 = jnp.float32
BF16 = jnp.bfloat16
MESH = pl.DeviceIdType.MESH
CZ = 128
ROWS, COLS = 8, 16
IL, JL = 48, 24
PX = IL * JL
NRES = 384
QS = PX // 128
PARTS = 3
HEADS, DH = 4, 32
STRIP = 3 * JL
LINE0 = 80
LOG2E = 1.4426950408889634
SCALE = DH ** -0.5


def normalize(v):
    mean = jnp.mean(v, axis=-1, keepdims=True)
    c = v - mean
    spread = jnp.mean(c * c, axis=-1, keepdims=True)
    return c * lax.rsqrt(spread + 1e-05)


def dot(a, b, dims=((1,), (0,))):
    return lax.dot_general(a, b, (dims, ((), ())), preferred_element_type=F32)


def repeat(n, body, first=0):
    def step(i, carry):
        body(i)
        return carry

    lax.fori_loop(first, n, step, 0)


def to_peers(axis, r, s, act):
    n, me = (ROWS, r) if axis == "row" else (COLS, s)

    def one(d):
        p = jnp.bitwise_xor(me, d)
        act(p, (p, s) if axis == "row" else (r, p))

    repeat(n, one, 1)


def scatter_to(axis, src, dst, send, recv, r, s):
    to_peers(axis, r, s, lambda p, device: pltpu.make_async_remote_copy(
        src_ref=src(p), dst_ref=dst, send_sem=send, recv_sem=recv, device_id=device, device_id_type=MESH
    ).start())


def drain(ref, sem):
    pltpu.make_async_copy(ref, ref, sem).wait()


def three(a):
    return pl.ds(3 * a, 3)


class Triangle:
    SHAPES = [
        ((ROWS, QS, 32, 128), BF16), ((ROWS, QS, 32, 128), BF16),
        ((COLS, QS, 16, 128), BF16), ((COLS, QS, 16, 128), BF16),
        ((COLS, PARTS, 32, 128), BF16), ((COLS, PARTS, 32, 128), BF16),
        ((ROWS, QS, 16, 128), BF16), ((ROWS, QS, 16, 128), BF16),
    ]

    def __init__(self, t, x, nb, mask, weights, bufs, stage, left, right, sends, recvs, r, s):
        self.t, self.x, self.nb, self.mask, self.r, self.s = t, x, nb, mask, r, s
        self.proj, self.gate, self.out = weights
        self.s1, self.r1, self.s2, self.r2, self.s3, self.r3, self.s4, self.r4 = bufs
        self.stage, self.left, self.right, self.sends, self.recvs = stage, left, right, sends, recvs

    def side(self, a):
        r, s = self.r, self.s

        def chunk(i, _):
            q = 3 * a + i
            rows = pl.ds(pl.multiple_of(q * 128, 128), 128)
            n = normalize(self.x[rows, :]).astype(BF16)
            self.nb[rows, :] = n
            p = dot(n, self.proj[self.t])
            m = self.mask[pl.ds(q, 1), :]
            for k in range(2):
                v = jax.nn.sigmoid(p[:, (2 * k + 1) * CZ:(2 * k + 2) * CZ]) * p[:, 2 * k * CZ:(2 * k + 1) * CZ]
                v = (v.T * m).astype(BF16)
                for p_ in range(ROWS):
                    self.s1[p_, q, 16 * k:16 * k + 16, :] = v[16 * p_:16 * p_ + 16]
            return 0

        lax.fori_loop(0, 3, chunk, 0)
        scatter_to("row", lambda p: self.s1.at[p, three(a)], self.r1.at[r, three(a)], self.sends.at[0], self.recvs.at[0, a], r, s)
        self.r1[r, three(a)] = self.s1[r, three(a)]

    def relay(self, a):
        r, s, mid = self.r, self.s, self.stage
        drain(self.r1.at[pl.ds(0, ROWS - 1), three(a)], self.recvs.at[0, a])

        def chunk(i, _):
            q = 3 * a + i
            for p in range(ROWS):
                v = self.r1[p, q].astype(F32)
                for k in range(2):
                    mid[pl.ds(i * 256 + k * 8 + p, 16, stride=16), :] = v[16 * k:16 * k + 16]
            for c in range(16):
                self.s2[c, q] = mid[pl.ds(pl.multiple_of(i * 256 + c * 16, 16), 16), :].astype(BF16)
            return 0

        lax.fori_loop(0, 3, chunk, 0)
        scatter_to("col", lambda p: self.s2.at[p, three(a)], self.r2.at[s, three(a)], self.sends.at[1], self.recvs.at[1, a], r, s)
        self.r2[s, three(a)] = self.s2[s, three(a)]

    def gather(self, a):
        f = self.stage
        drain(self.r2.at[pl.ds(0, COLS - 1), three(a)], self.recvs.at[1, a])
        for i in range(3):
            for p in range(COLS):
                f[i * 256 + p * 16:i * 256 + p * 16 + 16, :] = self.r2[p, 3 * a + i].astype(F32)
        for k, ref in enumerate((self.left, self.right)):
            v = [jnp.concatenate([f[pl.ds(i * 256 + k * 8 + p, COLS, stride=16), :] for i in range(3)], axis=1) for p in range(ROWS)]
            for b in range(8):
                row = jnp.concatenate([u[:, IL * b:IL * (b + 1)] for u in v], axis=1)
                for i in range(3):
                    ref[pl.ds(i * NRES + 8 * a + b, COLS, stride=JL), :] = row[:, 128 * i:128 * (i + 1)]

    def multiply(self):
        lf, rt = (jnp.concatenate([ref[pl.ds(i * NRES, NRES), :] for i in range(3)], axis=1).astype(BF16) for ref in (self.left, self.right))
        prod = dot(rt, lf, ((0,), (0,))) if self.t == 0 else dot(rt, lf, ((1,), (1,)))
        for i in range(3):
            self.left[pl.ds(i * NRES, NRES), :] = prod[:, 128 * i:128 * (i + 1)]

    def give(self, a):
        r, s = self.r, self.s
        for p in range(COLS):
            v = [self.left[pl.ds(i * NRES + JL * p + 8 * a, 8), :] for i in range(3)]
            self.s3[p, a] = jnp.concatenate(v + [jnp.zeros((8, 128), F32)], axis=0).astype(BF16)
        scatter_to("col", lambda p: self.s3.at[p, a], self.r3.at[s, a], self.sends.at[2], self.recvs.at[2, a], r, s)
        self.r3[s, a] = self.s3[s, a]

    def relay_back(self, a):
        r, s, f = self.r, self.s, self.stage
        drain(self.r3.at[pl.ds(0, COLS - 1), a], self.recvs.at[2, a])
        for c in range(COLS):
            f[c * 32:c * 32 + 32, :] = self.r3[c, a].astype(F32)
        v = [jnp.concatenate([f[pl.ds(i * 8 + b, 16, stride=32), :] for i in range(3)], axis=1) for b in range(8)]
        for p in range(ROWS):
            row = jnp.concatenate([u[:, IL * p:IL * (p + 1)] for u in v], axis=1).astype(BF16)
            for i in range(3):
                self.s4[p, 3 * a + i] = row[:, 128 * i:128 * (i + 1)]
        scatter_to("row", lambda p: self.s4.at[p, three(a)], self.r4.at[r, three(a)], self.sends.at[3], self.recvs.at[3, a], r, s)
        self.r4[r, three(a)] = self.s4[r, three(a)]

    def finish(self, a):
        drain(self.r4.at[pl.ds(0, ROWS - 1), three(a)], self.recvs.at[3, a])

        def chunk(i, _):
            q = 3 * a + i
            rows = pl.ds(pl.multiple_of(q * 128, 128), 128)
            pr = jnp.concatenate([self.r4[p, q] for p in range(ROWS)], axis=0).astype(F32).T
            mixed = normalize(pr).astype(BF16)
            g = jax.nn.sigmoid(dot(self.nb[rows, :], self.gate[self.t]))
            self.x[rows, :] = self.x[rows, :] + g * dot(mixed, self.out[self.t])
            return 0

        lax.fori_loop(0, 3, chunk, 0)

    def middle(self):
        for step in (self.relay, self.gather):
            repeat(PARTS, step)
        self.multiply()
        for step in (self.give, self.relay_back):
            repeat(PARTS, step)

    def close(self):
        drain(self.s1.at[pl.ds(0, ROWS - 1)], self.sends.at[0])
        drain(self.s2.at[pl.ds(0, COLS - 1)], self.sends.at[1])
        drain(self.s3.at[pl.ds(0, COLS - 1)], self.sends.at[2])
        drain(self.s4.at[pl.ds(0, ROWS - 1)], self.sends.at[3])


class Attention:
    @staticmethod
    def shapes(t):
        msg = (COLS, LINE0, CZ) if t == 0 else (ROWS, 3 * IL, CZ)
        return [((ROWS, QS, HEADS, 128), F32), ((COLS * HEADS * STRIP, 128), F32)] + [(msg, BF16)] * 4

    SHARED = [
        ((PX, CZ), F32), ((PX, CZ), F32), ((PX, CZ), BF16), ((PX, CZ), BF16), ((PX, CZ), BF16), ((PX, CZ), F32),
        ((3 * CZ, NRES), BF16), ((PX, CZ), F32), ((3 * CZ, NRES), F32), ((PX, CZ), F32),
    ]

    def __init__(self, t, x, kb, weights, bufs, shared, sems, slots, r, s):
        self.t, self.x, self.kb, self.sems, self.slots, self.r, self.s = t, x, kb, sems, slots, r, s
        self.bias_w, self.w_project, self.w_out = weights
        self.p1, self.bias, self.msg, self.got, self.upd, self.back = bufs
        self.nf, self.line, self.qs, self.ks, self.vs, self.gs, self.vt, self.us, self.ot, self.acc = shared

    def chunk(self, a):
        t, r, s = self.t, self.r, self.s

        def one(i, _):
            q = 3 * a + i
            rows = pl.ds(pl.multiple_of(q * 128, 128), 128)
            n = normalize(self.x[rows, :])
            self.nf[rows, :] = n
            b8 = lax.dot_general(self.bias_w[t], n, (((1,), (1,)), ((), ())), precision=lax.Precision.HIGHEST, preferred_element_type=F32)
            self.p1[r, q] = (b8[:HEADS] + self.kb[t, pl.ds(q, 1), :]) * LOG2E
            return 0

        lax.fori_loop(0, 3, one, 0)
        mine = self.p1.at[r, three(a)]
        scatter_to("row", lambda p: mine, mine, self.sems.at[0], self.sems.at[4 + a], r, s)

    def at(self, dx, dy, dc):
        x, y, c = self.s // 8, (self.s % 8) // 2, self.s % 2
        return ((x + dx) % 2) * 8 + ((y + dy) % 4) * 2 + (c + dc) % 2

    def piece(self, slot, h):
        return self.bias.at[pl.ds(pl.multiple_of((slot * HEADS + h) * STRIP, 8), STRIP)]

    def arrived(self, d, h):
        drain(self.piece(self.at(*d), h), self.slots.at[self.at(*d), h])

    def pass_on(self, d, h, *targets):
        slot = self.at(*d)
        for target in targets:
            pltpu.make_async_remote_copy(
                src_ref=self.piece(slot, h), dst_ref=self.piece(slot, h), send_sem=self.sems.at[2], recv_sem=self.slots.at[slot, h],
                device_id=(self.r, self.at(*target)), device_id_type=MESH,
            ).start()

    def forward(self, h, step):
        across, up, down, other = (1, 0, 0), (0, 1, 0), (0, 3, 0), (0, 0, 1)
        if step == 0:
            self.arrived(across, h)
            self.pass_on(across, h, up, down, other)
            self.arrived(up, h)
            self.pass_on(up, h, other)
            self.arrived(down, h)
            self.pass_on(down, h, other)
            pl.when(h < 2)(lambda: self.pass_on(up, h, down))
            pl.when(h >= 2)(lambda: self.pass_on(down, h, up))
        elif step == 1:
            self.arrived((0, 2, 0), h)
            self.pass_on((0, 2, 0), h, across, other)
            for d in ((1, 1, 0), (1, 3, 0)):
                self.arrived(d, h)
                self.pass_on(d, h, other)
        elif step == 2:
            self.arrived((1, 2, 0), h)
            self.pass_on((1, 2, 0), h, other)
        else:
            repeat(8, lambda n: self.arrived((n // 4, n % 4, 1), h))

    def lines_out(self):
        if self.t == 0:
            for p in range(COLS):
                v = [self.nf[pl.ds(3 * p + u, JL, stride=IL), :] for u in range(3)]
                self.msg[p] = jnp.concatenate(v + [jnp.zeros((LINE0 - 72, CZ), F32)], axis=0).astype(BF16)
        else:
            for p in range(ROWS):
                self.msg[p] = self.nf[pl.ds(p * 3 * IL, 3 * IL), :].astype(BF16)
        scatter_to(self.axis(), lambda p: self.msg.at[p], self.got.at[self.me()], self.sems.at[1], self.sems.at[7], self.r, self.s)
        self.got[self.me()] = self.msg[self.me()]

    def axis(self):
        return "col" if self.t == 0 else "row"

    def me(self):
        return self.s if self.t == 0 else self.r

    def others(self):
        return pl.ds(0, COLS - 1 if self.t == 0 else ROWS - 1)

    def lines_in(self):
        drain(self.got.at[self.others()], self.sems.at[7])
        if self.t == 0:
            for p in range(COLS):
                v = self.got[p].astype(F32)
                for u in range(3):
                    self.line[pl.ds(u * NRES + p * JL, JL), :] = v[u * JL:(u + 1) * JL]
        else:
            for p in range(ROWS):
                for u in range(3):
                    self.line[pl.ds(u * NRES + p * IL, IL), :] = self.got[p, u * IL:(u + 1) * IL, :].astype(F32)

    def lay(self, a):
        drain(self.p1.at[pl.ds(0, ROWS - 1), three(a)], self.sems.at[4 + a])
        v = [jnp.concatenate([self.p1[p, 3 * a + i] for i in range(3)], axis=1) for p in range(ROWS)]
        for b in range(8):
            row = jnp.concatenate([u[:, IL * b:IL * (b + 1)] for u in v], axis=1)
            for i in range(3):
                self.bias[pl.ds(self.s * HEADS * STRIP + i * JL + 8 * a + b, HEADS, stride=STRIP), :] = row[:, 128 * i:128 * (i + 1)]

    def project(self, u):
        rows = pl.ds(u * NRES, NRES)
        p = dot(self.line[rows, :].astype(BF16), self.w_project[self.t])
        self.qs[rows, :] = p[:, :CZ].astype(BF16)
        self.ks[rows, :] = p[:, CZ:2 * CZ].astype(BF16)
        v = p[:, 2 * CZ:3 * CZ]
        if self.t == 0:
            self.vt[pl.ds(u * CZ, CZ), :] = v.T.astype(BF16)
        else:
            self.vs[rows, :] = v.astype(BF16)
        self.gs[rows, :] = jax.nn.sigmoid(p[:, 3 * CZ:])

    def weights_of(self, scores, bias):
        e = scores * (SCALE * LOG2E) + bias
        return jnp.exp2(e - jnp.max(e, axis=self.t, keepdims=True))

    def bias_rows(self, slot, h, i):
        return self.bias[pl.ds(pl.multiple_of((slot * HEADS + h) * STRIP + i * JL, 8), JL), :]

    def tile(self, u, h):
        keep = lax.broadcasted_iota(jnp.int32, (1, CZ), 1) // DH == h
        k = self.ks[pl.ds(u * NRES, NRES), :]
        if self.t == 0:
            vt = self.vt[pl.ds(pl.multiple_of(u * CZ + h * DH, DH), DH), :]
            for i in range(3):
                q = self.qs[pl.ds(u * NRES + i * 128, 128), :]
                q = jnp.where(keep, q, jnp.zeros_like(q))
                b = jnp.concatenate([self.bias_rows(p, h, i) for p in range(COLS)], axis=0)
                e = self.weights_of(dot(k, q, ((1,), (1,))), b)
                o = dot(vt, e.astype(BF16)) / jnp.sum(e, axis=0, keepdims=True)
                self.ot[pl.ds(pl.multiple_of(u * CZ + h * DH, DH), DH), pl.ds(i * 128, 128)] = o
        else:
            v = self.vs[pl.ds(u * NRES, NRES), :]
            k = jnp.where(keep, k, jnp.zeros_like(k))
            v = jnp.concatenate([jnp.where(keep, v, jnp.zeros_like(v)), jnp.ones_like(v)], axis=1)
            for i in range(4):
                rows = pl.ds(u * NRES + i * 96, 96)
                b = jnp.concatenate([
                    jnp.concatenate([self.bias_rows(4 * i + p, h, w) for p in range(4)], axis=0) for w in range(3)], axis=1)
                e = self.weights_of(dot(self.qs[rows, :], k, ((1,), (1,))), b)
                o = dot(e.astype(BF16), v)
                o = o[:, :CZ] / o[:, CZ:]
                self.acc[rows, :] = self.acc[rows, :] + o

    def merge(self, u):
        rows = pl.ds(u * NRES, NRES)
        att = self.ot[pl.ds(u * CZ, CZ), :].T if self.t == 0 else self.acc[rows, :]
        self.us[rows, :] = dot((self.gs[rows, :] * att).astype(BF16), self.w_out[self.t])

    def run(self):
        self.lines_out()
        repeat(PARTS, self.lay)
        repeat(HEADS, lambda h: self.pass_on((0, 0, 0), h, (1, 0, 0), (0, 1, 0), (0, 3, 0), (0, 0, 1)))
        self.lines_in()
        if self.t == 1:
            self.acc[...] = jnp.zeros_like(self.acc)
        for u in range(3):
            self.project(u)

        def head(turn):
            for step in range(3):
                h = turn - step
                pl.when((h >= 0) & (h < HEADS))(lambda: self.forward(h, step))

            @pl.when(turn >= 3)
            def _():
                self.forward(turn - 3, 3)
                for u in range(3):
                    self.tile(u, turn - 3)

        repeat(HEADS + 3, head)
        for u in range(3):
            self.merge(u)
        if self.t == 0:
            for p in range(COLS):
                v = [self.us[pl.ds(u * NRES + p * JL, JL), :] for u in range(3)]
                self.upd[p] = jnp.concatenate(v + [jnp.zeros((LINE0 - 72, CZ), F32)], axis=0).astype(BF16)
        else:
            for p in range(ROWS):
                for u in range(3):
                    self.upd[p, u * IL:(u + 1) * IL, :] = self.us[pl.ds(u * NRES + p * IL, IL), :].astype(BF16)
        scatter_to(self.axis(), lambda p: self.upd.at[p], self.back.at[self.me()], self.sems.at[3], self.sems.at[8], self.r, self.s)
        self.back[self.me()] = self.upd[self.me()]
        drain(self.back.at[self.others()], self.sems.at[8])
        if self.t == 0:
            for p in range(COLS):
                v = self.back[p].astype(F32)
                for u in range(3):
                    rows = pl.ds(3 * p + u, JL, stride=IL)
                    self.x[rows, :] = self.x[rows, :] + v[u * JL:(u + 1) * JL]
        else:
            for p in range(ROWS):
                rows = pl.ds(p * 3 * IL, 3 * IL)
                self.x[rows, :] = self.x[rows, :] + self.back[p].astype(F32)

    def close(self):
        drain(self.p1.at[pl.ds(0, ROWS - 1)], self.sems.at[0])
        drain(self.msg.at[self.others()], self.sems.at[1])
        drain(self.bias.at[pl.ds(0, 15 * HEADS * STRIP)], self.sems.at[2])
        drain(self.upd.at[self.others()], self.sems.at[3])


def kernel(pair, chain, live, table, proj, gate, out, att_w, bias_w, att_o, y, x, nb, mask, kb, stage, left, right, *more):
    r = lax.axis_index("row")
    s = lax.axis_index("col")
    barrier = pltpu.get_barrier_semaphore()
    for axis in ("row", "col"):
        to_peers(axis, r, s, lambda _, device: pl.semaphore_signal(barrier, inc=1, device_id=device, device_id_type=MESH))

    first, second = (r * IL).astype(F32), (s * JL).astype(F32)
    live_count = jnp.sum(live[...].astype(F32), axis=1, keepdims=True)
    begins = [jnp.sum((chain[...] < c).astype(F32), axis=1, keepdims=True) for c in (1, 2, 3)]

    def chain_of(residue):
        return sum((residue >= b).astype(F32) for b in begins)

    px = (lax.broadcasted_iota(jnp.int32, (QS, 128), 0) * 128 + lax.broadcasted_iota(jnp.int32, (QS, 128), 1)).astype(F32)
    jl = jnp.floor((px + 0.5) * (1.0 / IL))
    live_i = (first + px - IL * jl < live_count).astype(F32)
    live_j = (second + jl < live_count).astype(F32)
    mask[...] = live_i * live_j
    kb[0] = (live_j - 1.0) * 1e9
    kb[1] = (live_i - 1.0) * 1e9
    chain_i = chain_of(first + lax.broadcasted_iota(jnp.int32, (IL, CZ), 0).astype(F32))
    for j in range(JL):
        same = chain_i == chain_of(second + jnp.full((1, CZ), j, F32))
        x[pl.ds(j * IL, IL), :] = pair[pl.ds(j, IL, stride=JL), :] + jnp.where(same, table[1:2, :], table[0:1, :])

    more = list(more)

    def take(n):
        got, more[:] = more[:n], more[n:]
        return got

    tri_bufs = [take(8), take(8)]
    att_bufs = [take(6), take(6)]
    shared = take(len(Attention.SHARED))
    tri_send, tri_recv, att_sems, slots = take(4)
    tri = [Triangle(t, x, nb, mask, (proj, gate, out), tri_bufs[t], stage, left, right, tri_send.at[t], tri_recv.at[t], r, s) for t in range(2)]
    att = [Attention(t, x, kb, (bias_w, att_w, att_o), att_bufs[t], shared, att_sems.at[t], slots.at[t], r, s) for t in range(2)]

    pl.semaphore_wait(barrier, ROWS + COLS - 2)
    repeat(PARTS, tri[0].side)
    tri[0].middle()
    repeat(PARTS, lambda a: (tri[0].finish(a), tri[1].side(a)))
    tri[1].middle()
    repeat(PARTS, lambda a: (tri[1].finish(a), att[0].chunk(a)))
    att[0].run()
    repeat(PARTS, att[1].chunk)
    att[1].run()
    for j in range(JL):
        y[pl.ds(j, IL, stride=JL), :] = x[pl.ds(j * IL, IL), :]
    for part in tri + att:
        part.close()


def call(*args):
    vm = pl.BlockSpec(memory_space=pltpu.VMEM)
    shapes = [
        ((PX, CZ), F32), ((PX, CZ), BF16), ((QS, 128), F32), ((2, QS, 128), F32), ((3 * 256, 128), F32), ((3 * NRES, 128), F32),
        ((3 * NRES, 128), F32), *Triangle.SHAPES, *Triangle.SHAPES, *Attention.shapes(0), *Attention.shapes(1), *Attention.SHARED,
    ]
    return pl.pallas_call(
        kernel,
        out_shape=jax.ShapeDtypeStruct((PX, CZ), F32),
        in_specs=[vm] * len(args),
        out_specs=vm,
        scratch_shapes=[pltpu.VMEM(*shape) for shape in shapes] + [
            pltpu.SemaphoreType.DMA((2, 4)),
            pltpu.SemaphoreType.DMA((2, 4, PARTS)),
            pltpu.SemaphoreType.DMA((2, 9)),
            pltpu.SemaphoreType.DMA((2, COLS, HEADS)),
        ],
        compiler_params=pltpu.CompilerParams(collective_id=0, has_side_effects=True, vmem_limit_bytes=56 << 20),
    )(*args)


def local(pair_rep, chain_id, live_mask, chain_table, tri_proj, tri_gate, tri_out, att_project, att_bias, att_out):
    bias_w = jnp.pad(jnp.swapaxes(att_bias, 1, 2), ((0, 0), (0, 8 - HEADS), (0, 0)))
    pair_out = call(
        pair_rep.reshape(PX, CZ), chain_id.reshape(1, NRES), live_mask.reshape(1, NRES), chain_table, tri_proj, tri_gate, tri_out,
        att_project, bias_w, att_out,
    )
    return pair_out.reshape(pair_rep.shape)


def solution(mesh):
    return jax.shard_map(
        local,
        mesh=mesh,
        in_specs=(P("row", "col", None), P(), P(), P(), P(), P(), P(), P(), P(), P()),
        out_specs=P("row", "col", None),
        check_vma=False,
    )
```

```python
import jax
import jax.numpy as jnp
from jax import lax
from jax.sharding import PartitionSpec as P
from jax.experimental import pallas as pl
from jax.experimental.pallas import tpu as pltpu

F32 = jnp.float32
BF16 = jnp.bfloat16
MESH = pl.DeviceIdType.MESH
CZ = 128
ROWS, COLS = 8, 16
IL, JL = 48, 24
PX = IL * JL
NRES = 384
QS = PX // 128
PARTS = 3
HEADS, DH = 4, 32
STRIP = 3 * JL
LINE0 = 80
LOG2E = 1.4426950408889634
SCALE = DH ** -0.5


def normalize(v):
    mean = jnp.mean(v, axis=-1, keepdims=True)
    c = v - mean
    spread = jnp.mean(c * c, axis=-1, keepdims=True)
    return c * lax.rsqrt(spread + 1e-05)


def dot(a, b, dims=((1,), (0,))):
    return lax.dot_general(a, b, (dims, ((), ())), preferred_element_type=F32)


def repeat(n, body, first=0):
    def step(i, carry):
        body(i)
        return carry

    lax.fori_loop(first, n, step, 0)


def to_peers(axis, r, s, act):
    n, me = (ROWS, r) if axis == "row" else (COLS, s)

    def one(d):
        p = jnp.bitwise_xor(me, n - d)
        act(p, (p, s) if axis == "row" else (r, p))

    repeat(n, one, 1)


def scatter_to(axis, src, dst, send, recv, r, s):
    to_peers(axis, r, s, lambda p, device: pltpu.make_async_remote_copy(
        src_ref=src(p), dst_ref=dst, send_sem=send, recv_sem=recv, device_id=device, device_id_type=MESH
    ).start())


def drain(ref, sem):
    pltpu.make_async_copy(ref, ref, sem).wait()


def three(a):
    return pl.ds(3 * a, 3)


class Triangle:
    SHAPES = [
        ((ROWS, QS, 32, 128), BF16), ((ROWS, QS, 32, 128), BF16),
        ((COLS, QS, 16, 128), BF16), ((COLS, QS, 16, 128), BF16),
        ((COLS, PARTS, 32, 128), BF16), ((COLS, PARTS, 32, 128), BF16),
        ((ROWS, QS, 16, 128), BF16), ((ROWS, QS, 16, 128), BF16),
    ]

    def __init__(self, t, x, nb, mask, weights, bufs, stage, left, right, sends, recvs, r, s):
        self.t, self.x, self.nb, self.mask, self.r, self.s = t, x, nb, mask, r, s
        self.proj, self.gate, self.out = weights
        self.s1, self.r1, self.s2, self.r2, self.s3, self.r3, self.s4, self.r4 = bufs
        self.stage, self.left, self.right, self.sends, self.recvs = stage, left, right, sends, recvs

    def side(self, a):

        def chunk(i, _):
            q = 3 * a + i
            rows = pl.ds(pl.multiple_of(q * 128, 128), 128)
            n = normalize(self.x[rows, :]).astype(BF16)
            self.nb[rows, :] = n
            p = dot(n, self.proj[self.t])
            m = self.mask[pl.ds(q, 1), :]
            for k in range(2):
                v = jax.nn.sigmoid(p[:, (2 * k + 1) * CZ:(2 * k + 2) * CZ]) * p[:, 2 * k * CZ:(2 * k + 1) * CZ]
                v = (v.T * m).astype(BF16)
                for p_ in range(ROWS):
                    self.s1[p_, q, 16 * k:16 * k + 16, :] = v[16 * p_:16 * p_ + 16]
            return 0

        lax.fori_loop(0, 3, chunk, 0)

    def side_out(self, a):
        r, s = self.r, self.s
        scatter_to("row", lambda p: self.s1.at[p, three(a)], self.r1.at[r, three(a)], self.sends.at[0], self.recvs.at[0, a], r, s)
        self.r1[r, three(a)] = self.s1[r, three(a)]

    def relay(self, a):
        r, s, mid = self.r, self.s, self.stage
        drain(self.r1.at[pl.ds(0, ROWS - 1), three(a)], self.recvs.at[0, a])

        def chunk(i, _):
            q = 3 * a + i
            for p in range(ROWS):
                v = self.r1[p, q].astype(F32)
                for k in range(2):
                    mid[pl.ds(i * 256 + k * 8 + p, 16, stride=16), :] = v[16 * k:16 * k + 16]
            for c in range(16):
                self.s2[c, q] = mid[pl.ds(pl.multiple_of(i * 256 + c * 16, 16), 16), :].astype(BF16)
            return 0

        lax.fori_loop(0, 3, chunk, 0)
        scatter_to("col", lambda p: self.s2.at[p, three(a)], self.r2.at[s, three(a)], self.sends.at[1], self.recvs.at[1, a], r, s)
        self.r2[s, three(a)] = self.s2[s, three(a)]

    def gather(self, a):
        f = self.stage
        drain(self.r2.at[pl.ds(0, COLS - 1), three(a)], self.recvs.at[1, a])
        for i in range(3):
            for p in range(COLS):
                f[i * 256 + p * 16:i * 256 + p * 16 + 16, :] = self.r2[p, 3 * a + i].astype(F32)
        for k, ref in enumerate((self.left, self.right)):
            v = [jnp.concatenate([f[pl.ds(i * 256 + k * 8 + p, COLS, stride=16), :] for i in range(3)], axis=1) for p in range(ROWS)]
            for b in range(8):
                row = jnp.concatenate([u[:, IL * b:IL * (b + 1)] for u in v], axis=1)
                for i in range(3):
                    ref[pl.ds(i * NRES + 8 * a + b, COLS, stride=JL), :] = row[:, 128 * i:128 * (i + 1)]

    def multiply(self):
        lf, rt = (jnp.concatenate([ref[pl.ds(i * NRES, NRES), :] for i in range(3)], axis=1).astype(BF16) for ref in (self.left, self.right))
        prod = dot(rt, lf, ((0,), (0,))) if self.t == 0 else dot(rt, lf, ((1,), (1,)))
        for i in range(3):
            self.left[pl.ds(i * NRES, NRES), :] = prod[:, 128 * i:128 * (i + 1)]

    def give(self, a):
        r, s = self.r, self.s
        for p in range(COLS):
            v = [self.left[pl.ds(i * NRES + JL * p + 8 * a, 8), :] for i in range(3)]
            self.s3[p, a] = jnp.concatenate(v + [jnp.zeros((8, 128), F32)], axis=0).astype(BF16)
        scatter_to("col", lambda p: self.s3.at[p, a], self.r3.at[s, a], self.sends.at[2], self.recvs.at[2, a], r, s)
        self.r3[s, a] = self.s3[s, a]

    def relay_back(self, a):
        r, s, f = self.r, self.s, self.stage
        drain(self.r3.at[pl.ds(0, COLS - 1), a], self.recvs.at[2, a])
        for c in range(COLS):
            f[c * 32:c * 32 + 32, :] = self.r3[c, a].astype(F32)
        v = [jnp.concatenate([f[pl.ds(i * 8 + b, 16, stride=32), :] for i in range(3)], axis=1) for b in range(8)]
        for p in range(ROWS):
            row = jnp.concatenate([u[:, IL * p:IL * (p + 1)] for u in v], axis=1).astype(BF16)
            for i in range(3):
                self.s4[p, 3 * a + i] = row[:, 128 * i:128 * (i + 1)]
        scatter_to("row", lambda p: self.s4.at[p, three(a)], self.r4.at[r, three(a)], self.sends.at[3], self.recvs.at[3, a], r, s)
        self.r4[r, three(a)] = self.s4[r, three(a)]

    def finish(self, a):
        drain(self.r4.at[pl.ds(0, ROWS - 1), three(a)], self.recvs.at[3, a])

        def chunk(i, _):
            q = 3 * a + i
            rows = pl.ds(pl.multiple_of(q * 128, 128), 128)
            pr = jnp.concatenate([self.r4[p, q] for p in range(ROWS)], axis=0).astype(F32).T
            mixed = normalize(pr).astype(BF16)
            g = jax.nn.sigmoid(dot(self.nb[rows, :], self.gate[self.t]))
            self.x[rows, :] = self.x[rows, :] + g * dot(mixed, self.out[self.t])
            return 0

        lax.fori_loop(0, 3, chunk, 0)

    def middle(self):
        for step in (self.relay, self.gather):
            repeat(PARTS, step)
        self.multiply()
        for step in (self.give, self.relay_back):
            repeat(PARTS, step)

    def close(self):
        drain(self.s1.at[pl.ds(0, ROWS - 1)], self.sends.at[0])
        drain(self.s2.at[pl.ds(0, COLS - 1)], self.sends.at[1])
        drain(self.s3.at[pl.ds(0, COLS - 1)], self.sends.at[2])
        drain(self.s4.at[pl.ds(0, ROWS - 1)], self.sends.at[3])


class Attention:
    @staticmethod
    def shapes(t):
        msg = (COLS, LINE0, CZ) if t == 0 else (ROWS, 3 * IL, CZ)
        return [((ROWS, QS, HEADS, 128), F32), ((COLS * HEADS * STRIP, 128), F32)] + [(msg, BF16)] * 4

    SHARED = [
        ((PX, CZ), F32), ((PX, CZ), F32), ((PX, CZ), BF16), ((PX, CZ), BF16), ((PX, CZ), BF16), ((PX, CZ), F32),
        ((3 * CZ, NRES), BF16), ((PX, CZ), F32), ((3 * CZ, NRES), F32), ((PX, CZ), F32),
    ]

    def __init__(self, t, x, kb, weights, bufs, shared, sems, slots, r, s):
        self.t, self.x, self.kb, self.sems, self.slots, self.r, self.s = t, x, kb, sems, slots, r, s
        self.bias_w, self.w_project, self.w_out = weights
        self.p1, self.bias, self.msg, self.got, self.upd, self.back = bufs
        self.nf, self.line, self.qs, self.ks, self.vs, self.gs, self.vt, self.us, self.ot, self.acc = shared

    def chunk(self, a):
        t, r, s = self.t, self.r, self.s

        def one(i, _):
            q = 3 * a + i
            rows = pl.ds(pl.multiple_of(q * 128, 128), 128)
            n = normalize(self.x[rows, :])
            self.nf[rows, :] = n
            b8 = lax.dot_general(self.bias_w[t], n, (((1,), (1,)), ((), ())), precision=lax.Precision.HIGHEST, preferred_element_type=F32)
            self.p1[r, q] = (b8[:HEADS] + self.kb[t, pl.ds(q, 1), :]) * LOG2E
            return 0

        lax.fori_loop(0, 3, one, 0)
        mine = self.p1.at[r, three(a)]
        scatter_to("row", lambda p: mine, mine, self.sems.at[0], self.sems.at[4 + a], r, s)

    def at(self, dx, dy, dc):
        x, y, c = self.s // 8, (self.s % 8) // 2, self.s % 2
        return ((x + dx) % 2) * 8 + ((y + dy) % 4) * 2 + (c + dc) % 2

    def piece(self, slot, h):
        return self.bias.at[pl.ds(pl.multiple_of((slot * HEADS + h) * STRIP, 8), STRIP)]

    def arrived(self, d, h):
        drain(self.piece(self.at(*d), h), self.slots.at[self.at(*d), h])

    def pass_on(self, d, h, *targets):
        slot = self.at(*d)
        for target in targets:
            pltpu.make_async_remote_copy(
                src_ref=self.piece(slot, h), dst_ref=self.piece(slot, h), send_sem=self.sems.at[2], recv_sem=self.slots.at[slot, h],
                device_id=(self.r, self.at(*target)), device_id_type=MESH,
            ).start()

    def forward(self, h, step):
        across, up, down, other = (1, 0, 0), (0, 1, 0), (0, 3, 0), (0, 0, 1)
        if step == 0:
            self.arrived(across, h)
            self.pass_on(across, h, up, down, other)
            self.arrived(up, h)
            self.pass_on(up, h, other)
            self.arrived(down, h)
            self.pass_on(down, h, other)
            pl.when(h < 2)(lambda: self.pass_on(up, h, down))
            pl.when(h >= 2)(lambda: self.pass_on(down, h, up))
        elif step == 1:
            self.arrived((0, 2, 0), h)
            self.pass_on((0, 2, 0), h, across, other)
            for d in ((1, 1, 0), (1, 3, 0)):
                self.arrived(d, h)
                self.pass_on(d, h, other)
        elif step == 2:
            self.arrived((1, 2, 0), h)
            self.pass_on((1, 2, 0), h, other)
        else:
            repeat(8, lambda n: self.arrived((n // 4, n % 4, 1), h))

    def lines_out(self):
        if self.t == 0:
            for p in range(COLS):
                v = [self.nf[pl.ds(3 * p + u, JL, stride=IL), :] for u in range(3)]
                self.msg[p] = jnp.concatenate(v + [jnp.zeros((LINE0 - 72, CZ), F32)], axis=0).astype(BF16)
        else:
            for p in range(ROWS):
                self.msg[p] = self.nf[pl.ds(p * 3 * IL, 3 * IL), :].astype(BF16)
        scatter_to(self.axis(), lambda p: self.msg.at[p], self.got.at[self.me()], self.sems.at[1], self.sems.at[7], self.r, self.s)
        self.got[self.me()] = self.msg[self.me()]

    def axis(self):
        return "col" if self.t == 0 else "row"

    def me(self):
        return self.s if self.t == 0 else self.r

    def others(self):
        return pl.ds(0, COLS - 1 if self.t == 0 else ROWS - 1)

    def lines_in(self):
        drain(self.got.at[self.others()], self.sems.at[7])
        if self.t == 0:
            for p in range(COLS):
                v = self.got[p].astype(F32)
                for u in range(3):
                    self.line[pl.ds(u * NRES + p * JL, JL), :] = v[u * JL:(u + 1) * JL]
        else:
            for p in range(ROWS):
                for u in range(3):
                    self.line[pl.ds(u * NRES + p * IL, IL), :] = self.got[p, u * IL:(u + 1) * IL, :].astype(F32)

    def lay(self, a):
        drain(self.p1.at[pl.ds(0, ROWS - 1), three(a)], self.sems.at[4 + a])
        v = [jnp.concatenate([self.p1[p, 3 * a + i] for i in range(3)], axis=1) for p in range(ROWS)]
        for b in range(8):
            row = jnp.concatenate([u[:, IL * b:IL * (b + 1)] for u in v], axis=1)
            for i in range(3):
                self.bias[pl.ds(self.s * HEADS * STRIP + i * JL + 8 * a + b, HEADS, stride=STRIP), :] = row[:, 128 * i:128 * (i + 1)]

    def project(self, u):
        rows = pl.ds(u * NRES, NRES)
        p = dot(self.line[rows, :].astype(BF16), self.w_project[self.t])
        self.qs[rows, :] = p[:, :CZ].astype(BF16)
        self.ks[rows, :] = p[:, CZ:2 * CZ].astype(BF16)
        v = p[:, 2 * CZ:3 * CZ]
        if self.t == 0:
            self.vt[pl.ds(u * CZ, CZ), :] = v.T.astype(BF16)
        else:
            self.vs[rows, :] = v.astype(BF16)
        self.gs[rows, :] = jax.nn.sigmoid(p[:, 3 * CZ:])

    def weights_of(self, scores, bias):
        e = scores * (SCALE * LOG2E) + bias
        return jnp.exp2(e - jnp.max(e, axis=self.t, keepdims=True))

    def bias_rows(self, slot, h, i):
        return self.bias[pl.ds(pl.multiple_of((slot * HEADS + h) * STRIP + i * JL, 8), JL), :]

    def tile(self, u, h):
        keep = lax.broadcasted_iota(jnp.int32, (1, CZ), 1) // DH == h
        k = self.ks[pl.ds(u * NRES, NRES), :]
        if self.t == 0:
            vt = self.vt[pl.ds(pl.multiple_of(u * CZ + h * DH, DH), DH), :]
            for i in range(3):
                q = self.qs[pl.ds(u * NRES + i * 128, 128), :]
                q = jnp.where(keep, q, jnp.zeros_like(q))
                b = jnp.concatenate([self.bias_rows(p, h, i) for p in range(COLS)], axis=0)
                e = self.weights_of(dot(k, q, ((1,), (1,))), b)
                o = dot(vt, e.astype(BF16)) / jnp.sum(e, axis=0, keepdims=True)
                self.ot[pl.ds(pl.multiple_of(u * CZ + h * DH, DH), DH), pl.ds(i * 128, 128)] = o
        else:
            v = self.vs[pl.ds(u * NRES, NRES), :]
            k = jnp.where(keep, k, jnp.zeros_like(k))
            v = jnp.concatenate([jnp.where(keep, v, jnp.zeros_like(v)), jnp.ones_like(v)], axis=1)
            for i in range(4):
                rows = pl.ds(u * NRES + i * 96, 96)
                b = jnp.concatenate([
                    jnp.concatenate([self.bias_rows(4 * i + p, h, w) for p in range(4)], axis=0) for w in range(3)], axis=1)
                e = self.weights_of(dot(self.qs[rows, :], k, ((1,), (1,))), b)
                o = dot(e.astype(BF16), v)
                o = o[:, :CZ] / o[:, CZ:]
                self.acc[rows, :] = self.acc[rows, :] + o

    def merge(self, u):
        rows = pl.ds(u * NRES, NRES)
        att = self.ot[pl.ds(u * CZ, CZ), :].T if self.t == 0 else self.acc[rows, :]
        self.us[rows, :] = dot((self.gs[rows, :] * att).astype(BF16), self.w_out[self.t])

    def run(self):
        self.lines_out()
        repeat(PARTS, self.lay)
        repeat(HEADS, lambda h: self.pass_on((0, 0, 0), h, (1, 0, 0), (0, 1, 0), (0, 3, 0), (0, 0, 1)))
        self.lines_in()
        if self.t == 1:
            self.acc[...] = jnp.zeros_like(self.acc)
        for u in range(3):
            self.project(u)

        def head(turn):
            for step in range(3):
                h = turn - step
                pl.when((h >= 0) & (h < HEADS))(lambda: self.forward(h, step))

            @pl.when(turn >= 3)
            def _():
                self.forward(turn - 3, 3)
                for u in range(3):
                    self.tile(u, turn - 3)

        repeat(HEADS + 3, head)
        for u in range(3):
            self.merge(u)
        if self.t == 0:
            for p in range(COLS):
                v = [self.us[pl.ds(u * NRES + p * JL, JL), :] for u in range(3)]
                self.upd[p] = jnp.concatenate(v + [jnp.zeros((LINE0 - 72, CZ), F32)], axis=0).astype(BF16)
        else:
            for p in range(ROWS):
                for u in range(3):
                    self.upd[p, u * IL:(u + 1) * IL, :] = self.us[pl.ds(u * NRES + p * IL, IL), :].astype(BF16)
        scatter_to(self.axis(), lambda p: self.upd.at[p], self.back.at[self.me()], self.sems.at[3], self.sems.at[8], self.r, self.s)
        self.back[self.me()] = self.upd[self.me()]
        drain(self.back.at[self.others()], self.sems.at[8])
        if self.t == 0:
            for p in range(COLS):
                v = self.back[p].astype(F32)
                for u in range(3):
                    rows = pl.ds(3 * p + u, JL, stride=IL)
                    self.x[rows, :] = self.x[rows, :] + v[u * JL:(u + 1) * JL]
        else:
            for p in range(ROWS):
                rows = pl.ds(p * 3 * IL, 3 * IL)
                self.x[rows, :] = self.x[rows, :] + self.back[p].astype(F32)

    def close(self):
        drain(self.p1.at[pl.ds(0, ROWS - 1)], self.sems.at[0])
        drain(self.msg.at[self.others()], self.sems.at[1])
        drain(self.bias.at[pl.ds(0, 15 * HEADS * STRIP)], self.sems.at[2])
        drain(self.upd.at[self.others()], self.sems.at[3])


def kernel(pair, chain, live, table, proj, gate, out, att_w, bias_c, att_o, y, x, nb, mask, kb, bias_w, stage, left, right, *more):
    r = lax.axis_index("row")
    s = lax.axis_index("col")
    barrier = pltpu.get_barrier_semaphore()
    for axis in ("row", "col"):
        to_peers(axis, r, s, lambda _, device: pl.semaphore_signal(barrier, inc=1, device_id=device, device_id_type=MESH))

    first, second = (r * IL).astype(F32), (s * JL).astype(F32)
    live_count = jnp.sum(live[...].reshape(1, NRES).astype(F32), axis=1, keepdims=True)
    begins = [jnp.sum((chain[...].reshape(1, NRES) < c).astype(F32), axis=1, keepdims=True) for c in (1, 2, 3)]

    def chain_of(residue):
        return sum((residue >= b).astype(F32) for b in begins)

    px = (lax.broadcasted_iota(jnp.int32, (QS, 128), 0) * 128 + lax.broadcasted_iota(jnp.int32, (QS, 128), 1)).astype(F32)
    jl = jnp.floor((px + 0.5) * (1.0 / IL))
    live_i = (first + px - IL * jl < live_count).astype(F32)
    live_j = (second + jl < live_count).astype(F32)
    mask[...] = live_i * live_j
    kb[0] = (live_j - 1.0) * 1e9
    kb[1] = (live_i - 1.0) * 1e9
    for t in range(2):
        wide = jnp.concatenate([bias_c[t], jnp.zeros((CZ, 128 - HEADS), F32)], axis=1)
        bias_w[t] = wide.T[:8]
    chain_i = chain_of(first + lax.broadcasted_iota(jnp.int32, (IL, CZ), 0).astype(F32))
    for j in range(JL):
        same = chain_i == chain_of(second + jnp.full((1, CZ), j, F32))
        x[pl.ds(j * IL, IL), :] = pair[pl.ds(j, IL, stride=JL), :] + jnp.where(same, table[1:2, :], table[0:1, :])

    more = list(more)

    def take(n):
        got, more[:] = more[:n], more[n:]
        return got

    tri_bufs = [take(8), take(8)]
    att_bufs = [take(6), take(6)]
    shared = take(len(Attention.SHARED))
    tri_send, tri_recv, att_sems, slots = take(4)
    tri = [Triangle(t, x, nb, mask, (proj, gate, out), tri_bufs[t], stage, left, right, tri_send.at[t], tri_recv.at[t], r, s) for t in range(2)]
    att = [Attention(t, x, kb, (bias_w, att_w, att_o), att_bufs[t], shared, att_sems.at[t], slots.at[t], r, s) for t in range(2)]

    tri[0].side(0)
    pl.semaphore_wait(barrier, ROWS + COLS - 2)
    tri[0].side_out(0)
    repeat(PARTS, lambda a: (tri[0].side(a), tri[0].side_out(a)), 1)
    tri[0].middle()
    repeat(PARTS, lambda a: (tri[0].finish(a), tri[1].side(a), tri[1].side_out(a)))
    tri[1].middle()
    repeat(PARTS, lambda a: (tri[1].finish(a), att[0].chunk(a)))
    att[0].run()
    repeat(PARTS, att[1].chunk)
    att[1].run()
    for j in range(JL):
        y[pl.ds(j, IL, stride=JL), :] = x[pl.ds(j * IL, IL), :]
    for part in tri + att:
        part.close()


def call(*args):
    vm = pl.BlockSpec(memory_space=pltpu.VMEM)
    shapes = [
        ((PX, CZ), F32), ((PX, CZ), BF16), ((QS, 128), F32), ((2, QS, 128), F32), ((2, 8, CZ), F32), ((3 * 256, 128), F32), ((3 * NRES, 128), F32),
        ((3 * NRES, 128), F32), *Triangle.SHAPES, *Triangle.SHAPES, *Attention.shapes(0), *Attention.shapes(1), *Attention.SHARED,
    ]
    return pl.pallas_call(
        kernel,
        out_shape=jax.ShapeDtypeStruct((PX, CZ), F32),
        in_specs=[vm] * len(args),
        out_specs=vm,
        scratch_shapes=[pltpu.VMEM(*shape) for shape in shapes] + [
            pltpu.SemaphoreType.DMA((2, 4)),
            pltpu.SemaphoreType.DMA((2, 4, PARTS)),
            pltpu.SemaphoreType.DMA((2, 9)),
            pltpu.SemaphoreType.DMA((2, COLS, HEADS)),
        ],
        compiler_params=pltpu.CompilerParams(collective_id=0, has_side_effects=True, vmem_limit_bytes=56 << 20),
    )(*args)


def local(pair_rep, chain_id, live_mask, chain_table, tri_proj, tri_gate, tri_out, att_project, att_bias, att_out):
    pair_out = call(
        pair_rep.reshape(PX, CZ), chain_id, live_mask, chain_table, tri_proj, tri_gate, tri_out,
        att_project, att_bias, att_out,
    )
    return pair_out.reshape(pair_rep.shape)


def solution(mesh):
    return jax.shard_map(
        local,
        mesh=mesh,
        in_specs=(P("row", "col", None), P(), P(), P(), P(), P(), P(), P(), P(), P()),
        out_specs=P("row", "col", None),
        check_vma=False,
    )
```

```python
import jax
import jax.numpy as jnp
from jax import lax
from jax.sharding import PartitionSpec as P
from jax.experimental import pallas as pl
from jax.experimental.pallas import tpu as pltpu

F32 = jnp.float32
BF16 = jnp.bfloat16
MESH = pl.DeviceIdType.MESH
CZ = 128
ROWS, COLS = 8, 16
IL, JL = 48, 24
PX = IL * JL
NRES = 384
QS = PX // 128
PARTS = 3
HEADS, DH = 4, 32
STRIP = 3 * JL
LINE0 = 80
LOG2E = 1.4426950408889634
SCALE = DH ** -0.5


def normalize(v):
    mean = jnp.mean(v, axis=-1, keepdims=True)
    c = v - mean
    spread = jnp.mean(c * c, axis=-1, keepdims=True)
    return c * lax.rsqrt(spread + 1e-05)


def sigmoid(v):
    return 0.5 * jnp.tanh(0.5 * v) + 0.5


def dot(a, b, dims=((1,), (0,))):
    return lax.dot_general(a, b, (dims, ((), ())), preferred_element_type=F32)


def repeat(n, body, first=0):
    def step(i, carry):
        body(i)
        return carry

    lax.fori_loop(first, n, step, 0)


def to_peers(axis, r, s, act):
    n, me = (ROWS, r) if axis == "row" else (COLS, s)

    def one(d):
        p = jnp.bitwise_xor(me, n - d)
        act(p, (p, s) if axis == "row" else (r, p))

    repeat(n, one, 1)


def scatter_to(axis, src, dst, send, recv, r, s):
    to_peers(axis, r, s, lambda p, device: pltpu.make_async_remote_copy(
        src_ref=src(p), dst_ref=dst, send_sem=send, recv_sem=recv, device_id=device, device_id_type=MESH
    ).start())


def drain(ref, sem):
    pltpu.make_async_copy(ref, ref, sem).wait()


def three(a):
    return pl.ds(3 * a, 3)


class Triangle:
    SHAPES = [
        ((ROWS, QS, 32, 128), BF16), ((ROWS, QS, 32, 128), BF16),
        ((COLS, QS, 16, 128), BF16), ((COLS, QS, 16, 128), BF16),
        ((COLS, PARTS, 32, 128), BF16), ((COLS, PARTS, 32, 128), BF16),
        ((ROWS, QS, 16, 128), BF16), ((ROWS, QS, 16, 128), BF16),
    ]

    def __init__(self, t, x, nb, mask, weights, bufs, stage, left, right, sends, recvs, r, s):
        self.t, self.x, self.nb, self.mask, self.r, self.s = t, x, nb, mask, r, s
        self.proj, self.gate, self.out = weights
        self.s1, self.r1, self.s2, self.r2, self.s3, self.r3, self.s4, self.r4 = bufs
        self.stage, self.left, self.right, self.sends, self.recvs = stage, left, right, sends, recvs

    def side(self, a):

        def chunk(i, _):
            q = 3 * a + i
            rows = pl.ds(pl.multiple_of(q * 128, 128), 128)
            n = normalize(self.x[rows, :]).astype(BF16)
            self.nb[rows, :] = n
            p = dot(n, self.proj[self.t])
            m = self.mask[pl.ds(q, 1), :]
            for k in range(2):
                v = sigmoid(p[:, (2 * k + 1) * CZ:(2 * k + 2) * CZ]) * p[:, 2 * k * CZ:(2 * k + 1) * CZ]
                v = (v.T * m).astype(BF16)
                for p_ in range(ROWS):
                    self.s1[p_, q, 16 * k:16 * k + 16, :] = v[16 * p_:16 * p_ + 16]
            return 0

        lax.fori_loop(0, 3, chunk, 0)

    def side_out(self, a):
        r, s = self.r, self.s
        scatter_to("row", lambda p: self.s1.at[p, three(a)], self.r1.at[r, three(a)], self.sends.at[0], self.recvs.at[0, a], r, s)
        self.r1[r, three(a)] = self.s1[r, three(a)]

    def relay(self, a):
        r, s, mid = self.r, self.s, self.stage
        drain(self.r1.at[pl.ds(0, ROWS - 1), three(a)], self.recvs.at[0, a])

        def chunk(i, _):
            q = 3 * a + i
            for p in range(ROWS):
                v = self.r1[p, q].astype(F32)
                for k in range(2):
                    mid[pl.ds(i * 256 + k * 8 + p, 16, stride=16), :] = v[16 * k:16 * k + 16]
            for c in range(16):
                self.s2[c, q] = mid[pl.ds(pl.multiple_of(i * 256 + c * 16, 16), 16), :].astype(BF16)
            return 0

        lax.fori_loop(0, 3, chunk, 0)
        scatter_to("col", lambda p: self.s2.at[p, three(a)], self.r2.at[s, three(a)], self.sends.at[1], self.recvs.at[1, a], r, s)
        self.r2[s, three(a)] = self.s2[s, three(a)]

    def gather(self, a):
        f = self.stage
        drain(self.r2.at[pl.ds(0, COLS - 1), three(a)], self.recvs.at[1, a])
        for i in range(3):
            for p in range(COLS):
                f[i * 256 + p * 16:i * 256 + p * 16 + 16, :] = self.r2[p, 3 * a + i].astype(F32)
        for k, ref in enumerate((self.left, self.right)):
            v = [jnp.concatenate([f[pl.ds(i * 256 + k * 8 + p, COLS, stride=16), :] for i in range(3)], axis=1) for p in range(ROWS)]
            for b in range(8):
                row = jnp.concatenate([u[:, IL * b:IL * (b + 1)] for u in v], axis=1)
                for i in range(3):
                    ref[pl.ds(i * NRES + 8 * a + b, COLS, stride=JL), :] = row[:, 128 * i:128 * (i + 1)]

    def multiply(self):
        lf, rt = (jnp.concatenate([ref[pl.ds(i * NRES, NRES), :] for i in range(3)], axis=1).astype(BF16) for ref in (self.left, self.right))
        prod = dot(rt, lf, ((0,), (0,))) if self.t == 0 else dot(rt, lf, ((1,), (1,)))
        for i in range(3):
            self.left[pl.ds(i * NRES, NRES), :] = prod[:, 128 * i:128 * (i + 1)]

    def give(self, a):
        r, s = self.r, self.s
        for p in range(COLS):
            v = [self.left[pl.ds(i * NRES + JL * p + 8 * a, 8), :] for i in range(3)]
            self.s3[p, a] = jnp.concatenate(v + [jnp.zeros((8, 128), F32)], axis=0).astype(BF16)
        scatter_to("col", lambda p: self.s3.at[p, a], self.r3.at[s, a], self.sends.at[2], self.recvs.at[2, a], r, s)
        self.r3[s, a] = self.s3[s, a]

    def relay_back(self, a):
        r, s, f = self.r, self.s, self.stage
        drain(self.r3.at[pl.ds(0, COLS - 1), a], self.recvs.at[2, a])
        for c in range(COLS):
            f[c * 32:c * 32 + 32, :] = self.r3[c, a].astype(F32)
        v = [jnp.concatenate([f[pl.ds(i * 8 + b, 16, stride=32), :] for i in range(3)], axis=1) for b in range(8)]
        for p in range(ROWS):
            row = jnp.concatenate([u[:, IL * p:IL * (p + 1)] for u in v], axis=1).astype(BF16)
            for i in range(3):
                self.s4[p, 3 * a + i] = row[:, 128 * i:128 * (i + 1)]
        scatter_to("row", lambda p: self.s4.at[p, three(a)], self.r4.at[r, three(a)], self.sends.at[3], self.recvs.at[3, a], r, s)
        self.r4[r, three(a)] = self.s4[r, three(a)]

    def finish(self, a):
        drain(self.r4.at[pl.ds(0, ROWS - 1), three(a)], self.recvs.at[3, a])

        def chunk(i, _):
            q = 3 * a + i
            rows = pl.ds(pl.multiple_of(q * 128, 128), 128)
            pr = jnp.concatenate([self.r4[p, q] for p in range(ROWS)], axis=0).astype(F32).T
            mixed = normalize(pr).astype(BF16)
            g = sigmoid(dot(self.nb[rows, :], self.gate[self.t]))
            self.x[rows, :] = self.x[rows, :] + g * dot(mixed, self.out[self.t])
            return 0

        lax.fori_loop(0, 3, chunk, 0)

    def middle(self):
        for step in (self.relay, self.gather):
            repeat(PARTS, step)
        self.multiply()
        for step in (self.give, self.relay_back):
            repeat(PARTS, step)

    def close(self):
        drain(self.s1.at[pl.ds(0, ROWS - 1)], self.sends.at[0])
        drain(self.s2.at[pl.ds(0, COLS - 1)], self.sends.at[1])
        drain(self.s3.at[pl.ds(0, COLS - 1)], self.sends.at[2])
        drain(self.s4.at[pl.ds(0, ROWS - 1)], self.sends.at[3])


class Attention:
    @staticmethod
    def shapes(t):
        msg = (COLS, LINE0, CZ) if t == 0 else (ROWS, 3 * IL, CZ)
        return [((ROWS, QS, HEADS, 128), F32), ((COLS * HEADS * STRIP, 128), F32)] + [(msg, BF16)] * 4

    SHARED = [
        ((PX, CZ), F32), ((PX, CZ), F32), ((PX, CZ), BF16), ((PX, CZ), BF16), ((PX, CZ), BF16), ((PX, CZ), F32),
        ((3 * CZ, NRES), BF16), ((PX, CZ), F32), ((3 * CZ, NRES), F32), ((PX, CZ), F32),
    ]

    def __init__(self, t, x, kb, weights, bufs, shared, sems, slots, r, s):
        self.t, self.x, self.kb, self.sems, self.slots, self.r, self.s = t, x, kb, sems, slots, r, s
        self.bias_w, self.w_project, self.w_out = weights
        self.p1, self.bias, self.msg, self.got, self.upd, self.back = bufs
        self.nf, self.line, self.qs, self.ks, self.vs, self.gs, self.vt, self.us, self.ot, self.acc = shared

    def chunk(self, a):
        t, r, s = self.t, self.r, self.s

        def one(i, _):
            q = 3 * a + i
            rows = pl.ds(pl.multiple_of(q * 128, 128), 128)
            n = normalize(self.x[rows, :])
            self.nf[rows, :] = n
            b8 = lax.dot_general(self.bias_w[t], n, (((1,), (1,)), ((), ())), precision=lax.Precision.HIGHEST, preferred_element_type=F32)
            self.p1[r, q] = (b8[:HEADS] + self.kb[t, pl.ds(q, 1), :]) * LOG2E
            return 0

        lax.fori_loop(0, 3, one, 0)
        mine = self.p1.at[r, three(a)]
        scatter_to("row", lambda p: mine, mine, self.sems.at[0], self.sems.at[4 + a], r, s)

    def at(self, dx, dy, dc):
        x, y, c = self.s // 8, (self.s % 8) // 2, self.s % 2
        return ((x + dx) % 2) * 8 + ((y + dy) % 4) * 2 + (c + dc) % 2

    def piece(self, slot, h):
        return self.bias.at[pl.ds(pl.multiple_of((slot * HEADS + h) * STRIP, 8), STRIP)]

    def arrived(self, d, h):
        drain(self.piece(self.at(*d), h), self.slots.at[self.at(*d), h])

    def pass_on(self, d, h, *targets):
        slot = self.at(*d)
        for target in targets:
            pltpu.make_async_remote_copy(
                src_ref=self.piece(slot, h), dst_ref=self.piece(slot, h), send_sem=self.sems.at[2], recv_sem=self.slots.at[slot, h],
                device_id=(self.r, self.at(*target)), device_id_type=MESH,
            ).start()

    def forward(self, h, step):
        across, up, down, other = (1, 0, 0), (0, 1, 0), (0, 3, 0), (0, 0, 1)
        if step == 0:
            self.arrived(up, h)
            self.pass_on(up, h, other)
            self.arrived(down, h)
            self.pass_on(down, h, other)
            pl.when(h < 2)(lambda: self.pass_on(up, h, down))
            pl.when(h >= 2)(lambda: self.pass_on(down, h, up))
            self.arrived(across, h)
            self.pass_on(across, h, up, down, other)
        elif step == 1:
            self.arrived((0, 2, 0), h)
            self.pass_on((0, 2, 0), h, across, other)
            for d in ((1, 1, 0), (1, 3, 0)):
                self.arrived(d, h)
                self.pass_on(d, h, other)
        elif step == 2:
            self.arrived((1, 2, 0), h)
            self.pass_on((1, 2, 0), h, other)
        else:
            repeat(8, lambda n: self.arrived((n // 4, n % 4, 1), h))

    def lines_out(self):
        if self.t == 0:
            for p in range(COLS):
                v = [self.nf[pl.ds(3 * p + u, JL, stride=IL), :] for u in range(3)]
                self.msg[p] = jnp.concatenate(v + [jnp.zeros((LINE0 - 72, CZ), F32)], axis=0).astype(BF16)
        else:
            for p in range(ROWS):
                self.msg[p] = self.nf[pl.ds(p * 3 * IL, 3 * IL), :].astype(BF16)
        scatter_to(self.axis(), lambda p: self.msg.at[p], self.got.at[self.me()], self.sems.at[1], self.sems.at[7], self.r, self.s)
        self.got[self.me()] = self.msg[self.me()]

    def axis(self):
        return "col" if self.t == 0 else "row"

    def me(self):
        return self.s if self.t == 0 else self.r

    def others(self):
        return pl.ds(0, COLS - 1 if self.t == 0 else ROWS - 1)

    def lines_in(self):
        drain(self.got.at[self.others()], self.sems.at[7])
        if self.t == 0:
            for p in range(COLS):
                v = self.got[p].astype(F32)
                for u in range(3):
                    self.line[pl.ds(u * NRES + p * JL, JL), :] = v[u * JL:(u + 1) * JL]
        else:
            for p in range(ROWS):
                for u in range(3):
                    self.line[pl.ds(u * NRES + p * IL, IL), :] = self.got[p, u * IL:(u + 1) * IL, :].astype(F32)

    def lay(self, a):
        drain(self.p1.at[pl.ds(0, ROWS - 1), three(a)], self.sems.at[4 + a])
        v = [jnp.concatenate([self.p1[p, 3 * a + i] for i in range(3)], axis=1) for p in range(ROWS)]
        for b in range(8):
            row = jnp.concatenate([u[:, IL * b:IL * (b + 1)] for u in v], axis=1)
            for i in range(3):
                self.bias[pl.ds(self.s * HEADS * STRIP + i * JL + 8 * a + b, HEADS, stride=STRIP), :] = row[:, 128 * i:128 * (i + 1)]

    def project(self, u):
        rows = pl.ds(u * NRES, NRES)
        p = dot(self.line[rows, :].astype(BF16), self.w_project[self.t])
        self.qs[rows, :] = p[:, :CZ].astype(BF16)
        self.ks[rows, :] = p[:, CZ:2 * CZ].astype(BF16)
        v = p[:, 2 * CZ:3 * CZ]
        if self.t == 0:
            self.vt[pl.ds(u * CZ, CZ), :] = v.T.astype(BF16)
        else:
            self.vs[rows, :] = v.astype(BF16)
        self.gs[rows, :] = sigmoid(p[:, 3 * CZ:])

    def weights_of(self, scores, bias):
        e = scores * (SCALE * LOG2E) + bias
        return jnp.exp2(e - jnp.max(e, axis=self.t, keepdims=True))

    def bias_rows(self, slot, h, i):
        return self.bias[pl.ds(pl.multiple_of((slot * HEADS + h) * STRIP + i * JL, 8), JL), :]

    def tile(self, u, h):
        keep = lax.broadcasted_iota(jnp.int32, (1, CZ), 1) // DH == h
        k = self.ks[pl.ds(u * NRES, NRES), :]
        if self.t == 0:
            vt = self.vt[pl.ds(pl.multiple_of(u * CZ + h * DH, DH), DH), :]
            for i in range(3):
                q = self.qs[pl.ds(u * NRES + i * 128, 128), :]
                q = jnp.where(keep, q, jnp.zeros_like(q))
                b = jnp.concatenate([self.bias_rows(p, h, i) for p in range(COLS)], axis=0)
                e = self.weights_of(dot(k, q, ((1,), (1,))), b)
                o = dot(vt, e.astype(BF16)) / jnp.sum(e, axis=0, keepdims=True)
                self.ot[pl.ds(pl.multiple_of(u * CZ + h * DH, DH), DH), pl.ds(i * 128, 128)] = o
        else:
            v = self.vs[pl.ds(u * NRES, NRES), :]
            k = jnp.where(keep, k, jnp.zeros_like(k))
            v = jnp.concatenate([jnp.where(keep, v, jnp.zeros_like(v)), jnp.ones_like(v)], axis=1)
            for i in range(4):
                rows = pl.ds(u * NRES + i * 96, 96)
                b = jnp.concatenate([
                    jnp.concatenate([self.bias_rows(4 * i + p, h, w) for p in range(4)], axis=0) for w in range(3)], axis=1)
                e = self.weights_of(dot(self.qs[rows, :], k, ((1,), (1,))), b)
                o = dot(e.astype(BF16), v)
                o = o[:, :CZ] / o[:, CZ:]
                self.acc[rows, :] = self.acc[rows, :] + o

    def merge(self, u):
        rows = pl.ds(u * NRES, NRES)
        att = self.ot[pl.ds(u * CZ, CZ), :].T if self.t == 0 else self.acc[rows, :]
        self.us[rows, :] = dot((self.gs[rows, :] * att).astype(BF16), self.w_out[self.t])

    def run(self):
        self.lines_out()
        repeat(PARTS, self.lay)
        repeat(HEADS, lambda h: self.pass_on((0, 0, 0), h, (0, 1, 0), (0, 3, 0), (1, 0, 0), (0, 0, 1)))
        self.lines_in()
        if self.t == 1:
            self.acc[...] = jnp.zeros_like(self.acc)
        for u in range(3):
            self.project(u)

        def head(turn):
            for step in range(3):
                h = turn - step
                pl.when((h >= 0) & (h < HEADS))(lambda: self.forward(h, step))

            @pl.when(turn >= 3)
            def _():
                self.forward(turn - 3, 3)
                for u in range(3):
                    self.tile(u, turn - 3)

        repeat(HEADS + 3, head)
        for u in range(3):
            self.merge(u)
        if self.t == 0:
            for p in range(COLS):
                v = [self.us[pl.ds(u * NRES + p * JL, JL), :] for u in range(3)]
                self.upd[p] = jnp.concatenate(v + [jnp.zeros((LINE0 - 72, CZ), F32)], axis=0).astype(BF16)
        else:
            for p in range(ROWS):
                for u in range(3):
                    self.upd[p, u * IL:(u + 1) * IL, :] = self.us[pl.ds(u * NRES + p * IL, IL), :].astype(BF16)
        scatter_to(self.axis(), lambda p: self.upd.at[p], self.back.at[self.me()], self.sems.at[3], self.sems.at[8], self.r, self.s)
        self.back[self.me()] = self.upd[self.me()]
        drain(self.back.at[self.others()], self.sems.at[8])
        if self.t == 0:
            for p in range(COLS):
                v = self.back[p].astype(F32)
                for u in range(3):
                    rows = pl.ds(3 * p + u, JL, stride=IL)
                    self.x[rows, :] = self.x[rows, :] + v[u * JL:(u + 1) * JL]
        else:
            for p in range(ROWS):
                rows = pl.ds(p * 3 * IL, 3 * IL)
                self.x[rows, :] = self.x[rows, :] + self.back[p].astype(F32)

    def close(self):
        drain(self.p1.at[pl.ds(0, ROWS - 1)], self.sems.at[0])
        drain(self.msg.at[self.others()], self.sems.at[1])
        drain(self.bias.at[pl.ds(0, 15 * HEADS * STRIP)], self.sems.at[2])
        drain(self.upd.at[self.others()], self.sems.at[3])


def kernel(pair, chain, live, table, proj, gate, out, att_w, bias_c, att_o, y, x, nb, mask, kb, bias_w, stage, left, right, *more):
    r = lax.axis_index("row")
    s = lax.axis_index("col")
    barrier = pltpu.get_barrier_semaphore()
    for axis in ("row", "col"):
        to_peers(axis, r, s, lambda _, device: pl.semaphore_signal(barrier, inc=1, device_id=device, device_id_type=MESH))

    first, second = (r * IL).astype(F32), (s * JL).astype(F32)
    live_count = jnp.sum(live[...].reshape(1, NRES).astype(F32), axis=1, keepdims=True)
    begins = [jnp.sum((chain[...].reshape(1, NRES) < c).astype(F32), axis=1, keepdims=True) for c in (1, 2, 3)]

    def chain_of(residue):
        return sum((residue >= b).astype(F32) for b in begins)

    px = (lax.broadcasted_iota(jnp.int32, (QS, 128), 0) * 128 + lax.broadcasted_iota(jnp.int32, (QS, 128), 1)).astype(F32)
    jl = jnp.floor((px + 0.5) * (1.0 / IL))
    live_i = (first + px - IL * jl < live_count).astype(F32)
    live_j = (second + jl < live_count).astype(F32)
    mask[...] = live_i * live_j
    kb[0] = (live_j - 1.0) * 1e9
    kb[1] = (live_i - 1.0) * 1e9
    for t in range(2):
        wide = jnp.concatenate([bias_c[t], jnp.zeros((CZ, 128 - HEADS), F32)], axis=1)
        bias_w[t] = wide.T[:8]
    chain_i = chain_of(first + lax.broadcasted_iota(jnp.int32, (IL, CZ), 0).astype(F32))
    for j in range(JL):
        same = chain_i == chain_of(second + jnp.full((1, CZ), j, F32))
        x[pl.ds(j * IL, IL), :] = pair[pl.ds(j, IL, stride=JL), :] + jnp.where(same, table[1:2, :], table[0:1, :])

    more = list(more)

    def take(n):
        got, more[:] = more[:n], more[n:]
        return got

    tri_bufs = [take(8), take(8)]
    att_bufs = [take(6), take(6)]
    shared = take(len(Attention.SHARED))
    tri_send, tri_recv, att_sems, slots = take(4)
    tri = [Triangle(t, x, nb, mask, (proj, gate, out), tri_bufs[t], stage, left, right, tri_send.at[t], tri_recv.at[t], r, s) for t in range(2)]
    att = [Attention(t, x, kb, (bias_w, att_w, att_o), att_bufs[t], shared, att_sems.at[t], slots.at[t], r, s) for t in range(2)]

    tri[0].side(0)
    pl.semaphore_wait(barrier, ROWS + COLS - 2)
    tri[0].side_out(0)
    repeat(PARTS, lambda a: (tri[0].side(a), tri[0].side_out(a)), 1)
    tri[0].middle()
    repeat(PARTS, lambda a: (tri[0].finish(a), tri[1].side(a), tri[1].side_out(a)))
    tri[1].middle()
    repeat(PARTS, lambda a: (tri[1].finish(a), att[0].chunk(a)))
    att[0].run()
    repeat(PARTS, att[1].chunk)
    att[1].run()
    for j in range(JL):
        y[pl.ds(j, IL, stride=JL), :] = x[pl.ds(j * IL, IL), :]
    for part in tri + att:
        part.close()


def call(*args):
    vm = pl.BlockSpec(memory_space=pltpu.VMEM)
    shapes = [
        ((PX, CZ), F32), ((PX, CZ), BF16), ((QS, 128), F32), ((2, QS, 128), F32), ((2, 8, CZ), F32), ((3 * 256, 128), F32), ((3 * NRES, 128), F32),
        ((3 * NRES, 128), F32), *Triangle.SHAPES, *Triangle.SHAPES, *Attention.shapes(0), *Attention.shapes(1), *Attention.SHARED,
    ]
    return pl.pallas_call(
        kernel,
        out_shape=jax.ShapeDtypeStruct((PX, CZ), F32),
        in_specs=[vm] * len(args),
        out_specs=vm,
        scratch_shapes=[pltpu.VMEM(*shape) for shape in shapes] + [
            pltpu.SemaphoreType.DMA((2, 4)),
            pltpu.SemaphoreType.DMA((2, 4, PARTS)),
            pltpu.SemaphoreType.DMA((2, 9)),
            pltpu.SemaphoreType.DMA((2, COLS, HEADS)),
        ],
        compiler_params=pltpu.CompilerParams(collective_id=0, has_side_effects=True, vmem_limit_bytes=56 << 20),
    )(*args)


def local(pair_rep, chain_id, live_mask, chain_table, tri_proj, tri_gate, tri_out, att_project, att_bias, att_out):
    pair_out = call(
        pair_rep.reshape(PX, CZ), chain_id, live_mask, chain_table, tri_proj, tri_gate, tri_out,
        att_project, att_bias, att_out,
    )
    return pair_out.reshape(pair_rep.shape)


def solution(mesh):
    return jax.shard_map(
        local,
        mesh=mesh,
        in_specs=(P("row", "col", None), P(), P(), P(), P(), P(), P(), P(), P(), P()),
        out_specs=P("row", "col", None),
        check_vma=False,
    )
```

```python
import jax
import jax.numpy as jnp
from jax import lax
from jax.sharding import PartitionSpec as P
from jax.experimental import pallas as pl
from jax.experimental.pallas import tpu as pltpu

F32 = jnp.float32
BF16 = jnp.bfloat16
MESH = pl.DeviceIdType.MESH
CZ = 128
ROWS, COLS = 8, 16
IL, JL = 48, 24
PX = IL * JL
NRES = 384
QS = PX // 128
PARTS = 3
HEADS, DH = 4, 32
STRIP = 3 * JL
LINE0 = 80
LOG2E = 1.4426950408889634
SCALE = DH ** -0.5


def normalize(v):
    mean = jnp.mean(v, axis=-1, keepdims=True)
    c = v - mean
    spread = jnp.mean(c * c, axis=-1, keepdims=True)
    return c * lax.rsqrt(spread + 1e-05)


def sigmoid(v):
    return 0.5 * jnp.tanh(0.5 * v) + 0.5


def dot(a, b, dims=((1,), (0,))):
    return lax.dot_general(a, b, (dims, ((), ())), preferred_element_type=F32)


def repeat(n, body, first=0, unroll=1):
    def step(i, carry):
        body(i)
        return carry

    lax.fori_loop(first, n, step, 0, unroll=unroll)


def to_peers(axis, r, s, act):
    n, me = (ROWS, r) if axis == "row" else (COLS, s)

    def one(d):
        p = jnp.bitwise_xor(me, n - d)
        act(p, (p, s) if axis == "row" else (r, p))

    repeat(n, one, 1, 7 if n == ROWS else 5)


def scatter_to(axis, src, dst, send, recv, r, s):
    to_peers(axis, r, s, lambda p, device: pltpu.make_async_remote_copy(
        src_ref=src(p), dst_ref=dst, send_sem=send, recv_sem=recv, device_id=device, device_id_type=MESH
    ).start())


def drain(ref, sem):
    pltpu.make_async_copy(ref, ref, sem).wait()


def three(a):
    return pl.ds(3 * a, 3)


class Triangle:
    SHAPES = [
        ((ROWS, QS, 32, 128), BF16), ((ROWS, QS, 32, 128), BF16),
        ((COLS, QS, 16, 128), BF16), ((COLS, QS, 16, 128), BF16),
        ((COLS, PARTS, 32, 128), BF16), ((COLS, PARTS, 32, 128), BF16),
        ((ROWS, QS, 16, 128), BF16), ((ROWS, QS, 16, 128), BF16),
    ]

    def __init__(self, t, x, nb, mask, weights, bufs, stage, left, right, sends, recvs, r, s):
        self.t, self.x, self.nb, self.mask, self.r, self.s = t, x, nb, mask, r, s
        self.proj, self.gate, self.out = weights
        self.s1, self.r1, self.s2, self.r2, self.s3, self.r3, self.s4, self.r4 = bufs
        self.stage, self.left, self.right, self.sends, self.recvs = stage, left, right, sends, recvs

    def side(self, a):

        def chunk(i, _):
            q = 3 * a + i
            rows = pl.ds(pl.multiple_of(q * 128, 128), 128)
            n = normalize(self.x[rows, :]).astype(BF16)
            self.nb[rows, :] = n
            p = dot(n, self.proj[self.t])
            m = self.mask[pl.ds(q, 1), :]
            for k in range(2):
                v = sigmoid(p[:, (2 * k + 1) * CZ:(2 * k + 2) * CZ]) * p[:, 2 * k * CZ:(2 * k + 1) * CZ]
                v = (v.T * m).astype(BF16)
                for p_ in range(ROWS):
                    self.s1[p_, q, 16 * k:16 * k + 16, :] = v[16 * p_:16 * p_ + 16]
            return 0

        lax.fori_loop(0, 3, chunk, 0)

    def side_out(self, a):
        r, s = self.r, self.s
        scatter_to("row", lambda p: self.s1.at[p, three(a)], self.r1.at[r, three(a)], self.sends.at[0], self.recvs.at[0, a], r, s)
        self.r1[r, three(a)] = self.s1[r, three(a)]

    def relay(self, a):
        r, s, mid = self.r, self.s, self.stage
        drain(self.r1.at[pl.ds(0, ROWS - 1), three(a)], self.recvs.at[0, a])

        def chunk(i, _):
            q = 3 * a + i
            for p in range(ROWS):
                v = self.r1[p, q].astype(F32)
                for k in range(2):
                    mid[pl.ds(i * 256 + k * 8 + p, 16, stride=16), :] = v[16 * k:16 * k + 16]
            for c in range(16):
                self.s2[c, q] = mid[pl.ds(pl.multiple_of(i * 256 + c * 16, 16), 16), :].astype(BF16)
            return 0

        lax.fori_loop(0, 3, chunk, 0)
        scatter_to("col", lambda p: self.s2.at[p, three(a)], self.r2.at[s, three(a)], self.sends.at[1], self.recvs.at[1, a], r, s)
        self.r2[s, three(a)] = self.s2[s, three(a)]

    def gather(self, a):
        f = self.stage
        drain(self.r2.at[pl.ds(0, COLS - 1), three(a)], self.recvs.at[1, a])
        for i in range(3):
            for p in range(COLS):
                f[i * 256 + p * 16:i * 256 + p * 16 + 16, :] = self.r2[p, 3 * a + i].astype(F32)
        for k, ref in enumerate((self.left, self.right)):
            v = [jnp.concatenate([f[pl.ds(i * 256 + k * 8 + p, COLS, stride=16), :] for i in range(3)], axis=1) for p in range(ROWS)]
            for b in range(8):
                row = jnp.concatenate([u[:, IL * b:IL * (b + 1)] for u in v], axis=1)
                for i in range(3):
                    ref[pl.ds(i * NRES + 8 * a + b, COLS, stride=JL), :] = row[:, 128 * i:128 * (i + 1)]

    def multiply(self):
        lf, rt = (jnp.concatenate([ref[pl.ds(i * NRES, NRES), :] for i in range(3)], axis=1).astype(BF16) for ref in (self.left, self.right))
        prod = dot(rt, lf, ((0,), (0,))) if self.t == 0 else dot(rt, lf, ((1,), (1,)))
        for i in range(3):
            self.left[pl.ds(i * NRES, NRES), :] = prod[:, 128 * i:128 * (i + 1)]

    def give(self, a):
        r, s = self.r, self.s
        for p in range(COLS):
            v = [self.left[pl.ds(i * NRES + JL * p + 8 * a, 8), :] for i in range(3)]
            self.s3[p, a] = jnp.concatenate(v + [jnp.zeros((8, 128), F32)], axis=0).astype(BF16)
        scatter_to("col", lambda p: self.s3.at[p, a], self.r3.at[s, a], self.sends.at[2], self.recvs.at[2, a], r, s)
        self.r3[s, a] = self.s3[s, a]

    def relay_back(self, a):
        r, s, f = self.r, self.s, self.stage
        drain(self.r3.at[pl.ds(0, COLS - 1), a], self.recvs.at[2, a])
        for c in range(COLS):
            f[c * 32:c * 32 + 32, :] = self.r3[c, a].astype(F32)
        v = [jnp.concatenate([f[pl.ds(i * 8 + b, 16, stride=32), :] for i in range(3)], axis=1) for b in range(8)]
        for p in range(ROWS):
            row = jnp.concatenate([u[:, IL * p:IL * (p + 1)] for u in v], axis=1).astype(BF16)
            for i in range(3):
                self.s4[p, 3 * a + i] = row[:, 128 * i:128 * (i + 1)]
        scatter_to("row", lambda p: self.s4.at[p, three(a)], self.r4.at[r, three(a)], self.sends.at[3], self.recvs.at[3, a], r, s)
        self.r4[r, three(a)] = self.s4[r, three(a)]

    def finish(self, a):
        drain(self.r4.at[pl.ds(0, ROWS - 1), three(a)], self.recvs.at[3, a])

        def chunk(i, _):
            q = 3 * a + i
            rows = pl.ds(pl.multiple_of(q * 128, 128), 128)
            pr = jnp.concatenate([self.r4[p, q] for p in range(ROWS)], axis=0).astype(F32).T
            mixed = normalize(pr).astype(BF16)
            g = sigmoid(dot(self.nb[rows, :], self.gate[self.t]))
            self.x[rows, :] = self.x[rows, :] + g * dot(mixed, self.out[self.t])
            return 0

        lax.fori_loop(0, 3, chunk, 0)

    def middle(self):
        for step in (self.relay, self.gather):
            repeat(PARTS, step)
        self.multiply()
        for step in (self.give, self.relay_back):
            repeat(PARTS, step)

    def close(self):
        drain(self.s1.at[pl.ds(0, ROWS - 1)], self.sends.at[0])
        drain(self.s2.at[pl.ds(0, COLS - 1)], self.sends.at[1])
        drain(self.s3.at[pl.ds(0, COLS - 1)], self.sends.at[2])
        drain(self.s4.at[pl.ds(0, ROWS - 1)], self.sends.at[3])


class Attention:
    @staticmethod
    def shapes(t):
        msg = (COLS, LINE0, CZ) if t == 0 else (ROWS, 3 * IL, CZ)
        return [((ROWS, QS, HEADS, 128), F32), ((COLS * HEADS * STRIP, 128), F32)] + [(msg, BF16)] * 4

    SHARED = [
        ((PX, CZ), F32), ((PX, CZ), F32), ((PX, CZ), BF16), ((PX, CZ), BF16), ((PX, CZ), BF16), ((PX, CZ), F32),
        ((3 * CZ, NRES), BF16), ((PX, CZ), F32), ((3 * CZ, NRES), F32), ((PX, CZ), F32),
    ]

    def __init__(self, t, x, kb, weights, bufs, shared, sems, slots, r, s):
        self.t, self.x, self.kb, self.sems, self.slots, self.r, self.s = t, x, kb, sems, slots, r, s
        self.bias_w, self.w_project, self.w_out = weights
        self.p1, self.bias, self.msg, self.got, self.upd, self.back = bufs
        self.nf, self.line, self.qs, self.ks, self.vs, self.gs, self.vt, self.us, self.ot, self.acc = shared

    def chunk(self, a):
        t, r, s = self.t, self.r, self.s

        def one(i, _):
            q = 3 * a + i
            rows = pl.ds(pl.multiple_of(q * 128, 128), 128)
            n = normalize(self.x[rows, :])
            self.nf[rows, :] = n
            b8 = lax.dot_general(self.bias_w[t], n, (((1,), (1,)), ((), ())), precision=lax.Precision.HIGHEST, preferred_element_type=F32)
            self.p1[r, q] = (b8[:HEADS] + self.kb[t, pl.ds(q, 1), :]) * LOG2E
            return 0

        lax.fori_loop(0, 3, one, 0)
        mine = self.p1.at[r, three(a)]
        scatter_to("row", lambda p: mine, mine, self.sems.at[0], self.sems.at[4 + a], r, s)

    def at(self, dx, dy, dc):
        x, y, c = self.s // 8, (self.s % 8) // 2, self.s % 2
        return ((x + dx) % 2) * 8 + ((y + dy) % 4) * 2 + (c + dc) % 2

    def piece(self, slot, h):
        return self.bias.at[pl.ds(pl.multiple_of((slot * HEADS + h) * STRIP, 8), STRIP)]

    def arrived(self, d, h):
        drain(self.piece(self.at(*d), h), self.slots.at[self.at(*d), h])

    def pass_on(self, d, h, *targets):
        slot = self.at(*d)
        for target in targets:
            pltpu.make_async_remote_copy(
                src_ref=self.piece(slot, h), dst_ref=self.piece(slot, h), send_sem=self.sems.at[2], recv_sem=self.slots.at[slot, h],
                device_id=(self.r, self.at(*target)), device_id_type=MESH,
            ).start()

    def forward(self, h, step):
        across, up, down, other = (1, 0, 0), (0, 1, 0), (0, 3, 0), (0, 0, 1)
        if step == 0:
            self.arrived(up, h)
            self.pass_on(up, h, other)
            self.arrived(down, h)
            self.pass_on(down, h, other)
            pl.when(h < 2)(lambda: self.pass_on(up, h, down))
            pl.when(h >= 2)(lambda: self.pass_on(down, h, up))
            self.arrived(across, h)
            self.pass_on(across, h, up, down, other)
        elif step == 1:
            self.arrived((0, 2, 0), h)
            self.pass_on((0, 2, 0), h, across, other)
            for d in ((1, 1, 0), (1, 3, 0)):
                self.arrived(d, h)
                self.pass_on(d, h, other)
        elif step == 2:
            self.arrived((1, 2, 0), h)
            self.pass_on((1, 2, 0), h, other)
        else:
            repeat(8, lambda n: self.arrived((n // 4, n % 4, 1), h))

    def lines_out(self):
        if self.t == 0:
            for p in range(COLS):
                v = [self.nf[pl.ds(3 * p + u, JL, stride=IL), :] for u in range(3)]
                self.msg[p] = jnp.concatenate(v + [jnp.zeros((LINE0 - 72, CZ), F32)], axis=0).astype(BF16)
        else:
            for p in range(ROWS):
                self.msg[p] = self.nf[pl.ds(p * 3 * IL, 3 * IL), :].astype(BF16)
        scatter_to(self.axis(), lambda p: self.msg.at[p], self.got.at[self.me()], self.sems.at[1], self.sems.at[7], self.r, self.s)
        self.got[self.me()] = self.msg[self.me()]

    def axis(self):
        return "col" if self.t == 0 else "row"

    def me(self):
        return self.s if self.t == 0 else self.r

    def others(self):
        return pl.ds(0, COLS - 1 if self.t == 0 else ROWS - 1)

    def lines_in(self):
        drain(self.got.at[self.others()], self.sems.at[7])
        if self.t == 0:
            for p in range(COLS):
                v = self.got[p].astype(F32)
                for u in range(3):
                    self.line[pl.ds(u * NRES + p * JL, JL), :] = v[u * JL:(u + 1) * JL]
        else:
            for p in range(ROWS):
                for u in range(3):
                    self.line[pl.ds(u * NRES + p * IL, IL), :] = self.got[p, u * IL:(u + 1) * IL, :].astype(F32)

    def lay(self, a):
        drain(self.p1.at[pl.ds(0, ROWS - 1), three(a)], self.sems.at[4 + a])
        v = [jnp.concatenate([self.p1[p, 3 * a + i] for i in range(3)], axis=1) for p in range(ROWS)]
        for b in range(8):
            row = jnp.concatenate([u[:, IL * b:IL * (b + 1)] for u in v], axis=1)
            for i in range(3):
                self.bias[pl.ds(self.s * HEADS * STRIP + i * JL + 8 * a + b, HEADS, stride=STRIP), :] = row[:, 128 * i:128 * (i + 1)]

    def project(self, u):
        rows = pl.ds(u * NRES, NRES)
        p = dot(self.line[rows, :].astype(BF16), self.w_project[self.t])
        self.qs[rows, :] = p[:, :CZ].astype(BF16)
        self.ks[rows, :] = p[:, CZ:2 * CZ].astype(BF16)
        v = p[:, 2 * CZ:3 * CZ]
        if self.t == 0:
            self.vt[pl.ds(u * CZ, CZ), :] = v.T.astype(BF16)
        else:
            self.vs[rows, :] = v.astype(BF16)
        self.gs[rows, :] = sigmoid(p[:, 3 * CZ:])

    def weights_of(self, scores, bias):
        e = scores * (SCALE * LOG2E) + bias
        return jnp.exp2(e - jnp.max(e, axis=self.t, keepdims=True))

    def bias_rows(self, slot, h, i):
        return self.bias[pl.ds(pl.multiple_of((slot * HEADS + h) * STRIP + i * JL, 8), JL), :]

    def tile(self, u, h):
        keep = lax.broadcasted_iota(jnp.int32, (1, CZ), 1) // DH == h
        k = self.ks[pl.ds(u * NRES, NRES), :]
        if self.t == 0:
            vt = self.vt[pl.ds(pl.multiple_of(u * CZ + h * DH, DH), DH), :]
            for i in range(3):
                q = self.qs[pl.ds(u * NRES + i * 128, 128), :]
                q = jnp.where(keep, q, jnp.zeros_like(q))
                b = jnp.concatenate([self.bias_rows(p, h, i) for p in range(COLS)], axis=0)
                e = self.weights_of(dot(k, q, ((1,), (1,))), b)
                o = dot(vt, e.astype(BF16)) / jnp.sum(e, axis=0, keepdims=True)
                self.ot[pl.ds(pl.multiple_of(u * CZ + h * DH, DH), DH), pl.ds(i * 128, 128)] = o
        else:
            v = self.vs[pl.ds(u * NRES, NRES), :]
            k = jnp.where(keep, k, jnp.zeros_like(k))
            v = jnp.concatenate([jnp.where(keep, v, jnp.zeros_like(v)), jnp.ones_like(v)], axis=1)
            for i in range(4):
                rows = pl.ds(u * NRES + i * 96, 96)
                b = jnp.concatenate([
                    jnp.concatenate([self.bias_rows(4 * i + p, h, w) for p in range(4)], axis=0) for w in range(3)], axis=1)
                e = self.weights_of(dot(self.qs[rows, :], k, ((1,), (1,))), b)
                o = dot(e.astype(BF16), v)
                o = o[:, :CZ] / o[:, CZ:]
                self.acc[rows, :] = self.acc[rows, :] + o

    def merge(self, u):
        rows = pl.ds(u * NRES, NRES)
        att = self.ot[pl.ds(u * CZ, CZ), :].T if self.t == 0 else self.acc[rows, :]
        self.us[rows, :] = dot((self.gs[rows, :] * att).astype(BF16), self.w_out[self.t])

    def run(self):
        self.lines_out()
        repeat(PARTS, self.lay)
        repeat(HEADS, lambda h: self.pass_on((0, 0, 0), h, (0, 1, 0), (0, 3, 0), (1, 0, 0), (0, 0, 1)))
        self.lines_in()
        if self.t == 1:
            self.acc[...] = jnp.zeros_like(self.acc)
        for u in range(3):
            self.project(u)

        def head(turn):
            for step in range(3):
                h = turn - step
                pl.when((h >= 0) & (h < HEADS))(lambda: self.forward(h, step))

            @pl.when(turn >= 3)
            def _():
                self.forward(turn - 3, 3)
                for u in range(3):
                    self.tile(u, turn - 3)

        repeat(HEADS + 3, head)
        for u in range(3):
            self.merge(u)
        if self.t == 0:
            for p in range(COLS):
                v = [self.us[pl.ds(u * NRES + p * JL, JL), :] for u in range(3)]
                self.upd[p] = jnp.concatenate(v + [jnp.zeros((LINE0 - 72, CZ), F32)], axis=0).astype(BF16)
        else:
            for p in range(ROWS):
                for u in range(3):
                    self.upd[p, u * IL:(u + 1) * IL, :] = self.us[pl.ds(u * NRES + p * IL, IL), :].astype(BF16)
        scatter_to(self.axis(), lambda p: self.upd.at[p], self.back.at[self.me()], self.sems.at[3], self.sems.at[8], self.r, self.s)
        self.back[self.me()] = self.upd[self.me()]
        drain(self.back.at[self.others()], self.sems.at[8])
        if self.t == 0:
            for p in range(COLS):
                v = self.back[p].astype(F32)
                for u in range(3):
                    rows = pl.ds(3 * p + u, JL, stride=IL)
                    self.x[rows, :] = self.x[rows, :] + v[u * JL:(u + 1) * JL]
        else:
            for p in range(ROWS):
                rows = pl.ds(p * 3 * IL, 3 * IL)
                self.x[rows, :] = self.x[rows, :] + self.back[p].astype(F32)

    def close(self):
        drain(self.p1.at[pl.ds(0, ROWS - 1)], self.sems.at[0])
        drain(self.msg.at[self.others()], self.sems.at[1])
        drain(self.bias.at[pl.ds(0, 15 * HEADS * STRIP)], self.sems.at[2])
        drain(self.upd.at[self.others()], self.sems.at[3])


def kernel(pair, chain, live, table, proj, gate, out, att_w, bias_c, att_o, y, x, nb, mask, kb, bias_w, stage, left, right, *more):
    r = lax.axis_index("row")
    s = lax.axis_index("col")
    barrier = pltpu.get_barrier_semaphore()
    for axis in ("row", "col"):
        to_peers(axis, r, s, lambda _, device: pl.semaphore_signal(barrier, inc=1, device_id=device, device_id_type=MESH))

    first, second = (r * IL).astype(F32), (s * JL).astype(F32)
    live_count = jnp.sum(live[...].reshape(1, NRES).astype(F32), axis=1, keepdims=True)
    begins = [jnp.sum((chain[...].reshape(1, NRES) < c).astype(F32), axis=1, keepdims=True) for c in (1, 2, 3)]

    def chain_of(residue):
        return sum((residue >= b).astype(F32) for b in begins)

    px = (lax.broadcasted_iota(jnp.int32, (QS, 128), 0) * 128 + lax.broadcasted_iota(jnp.int32, (QS, 128), 1)).astype(F32)
    jl = jnp.floor((px + 0.5) * (1.0 / IL))
    live_i = (first + px - IL * jl < live_count).astype(F32)
    live_j = (second + jl < live_count).astype(F32)
    mask[...] = live_i * live_j
    kb[0] = (live_j - 1.0) * 1e9
    kb[1] = (live_i - 1.0) * 1e9
    for t in range(2):
        wide = jnp.concatenate([bias_c[t], jnp.zeros((CZ, 128 - HEADS), F32)], axis=1)
        bias_w[t] = wide.T[:8]
    chain_i = chain_of(first + lax.broadcasted_iota(jnp.int32, (IL, CZ), 0).astype(F32))
    for j in range(JL):
        same = chain_i == chain_of(second + jnp.full((1, CZ), j, F32))
        x[pl.ds(j * IL, IL), :] = pair[pl.ds(j, IL, stride=JL), :] + jnp.where(same, table[1:2, :], table[0:1, :])

    more = list(more)

    def take(n):
        got, more[:] = more[:n], more[n:]
        return got

    tri_bufs = [take(8), take(8)]
    att_bufs = [take(6), take(6)]
    shared = take(len(Attention.SHARED))
    tri_send, tri_recv, att_sems, slots = take(4)
    tri = [Triangle(t, x, nb, mask, (proj, gate, out), tri_bufs[t], stage, left, right, tri_send.at[t], tri_recv.at[t], r, s) for t in range(2)]
    att = [Attention(t, x, kb, (bias_w, att_w, att_o), att_bufs[t], shared, att_sems.at[t], slots.at[t], r, s) for t in range(2)]

    tri[0].side(0)
    pl.semaphore_wait(barrier, ROWS + COLS - 2)
    tri[0].side_out(0)
    repeat(PARTS, lambda a: (tri[0].side(a), tri[0].side_out(a)), 1)
    tri[0].middle()
    repeat(PARTS, lambda a: (tri[0].finish(a), tri[1].side(a), tri[1].side_out(a)))
    tri[1].middle()
    repeat(PARTS, lambda a: (tri[1].finish(a), att[0].chunk(a)))
    att[0].run()
    repeat(PARTS, att[1].chunk)
    att[1].run()
    for j in range(JL):
        y[pl.ds(j, IL, stride=JL), :] = x[pl.ds(j * IL, IL), :]
    for part in tri + att:
        part.close()


def call(*args):
    vm = pl.BlockSpec(memory_space=pltpu.VMEM)
    shapes = [
        ((PX, CZ), F32), ((PX, CZ), BF16), ((QS, 128), F32), ((2, QS, 128), F32), ((2, 8, CZ), F32), ((3 * 256, 128), F32), ((3 * NRES, 128), F32),
        ((3 * NRES, 128), F32), *Triangle.SHAPES, *Triangle.SHAPES, *Attention.shapes(0), *Attention.shapes(1), *Attention.SHARED,
    ]
    return pl.pallas_call(
        kernel,
        out_shape=jax.ShapeDtypeStruct((PX, CZ), F32),
        in_specs=[vm] * len(args),
        out_specs=vm,
        scratch_shapes=[pltpu.VMEM(*shape) for shape in shapes] + [
            pltpu.SemaphoreType.DMA((2, 4)),
            pltpu.SemaphoreType.DMA((2, 4, PARTS)),
            pltpu.SemaphoreType.DMA((2, 9)),
            pltpu.SemaphoreType.DMA((2, COLS, HEADS)),
        ],
        compiler_params=pltpu.CompilerParams(collective_id=0, has_side_effects=True, vmem_limit_bytes=56 << 20),
    )(*args)


def local(pair_rep, chain_id, live_mask, chain_table, tri_proj, tri_gate, tri_out, att_project, att_bias, att_out):
    pair_out = call(
        pair_rep.reshape(PX, CZ), chain_id, live_mask, chain_table, tri_proj, tri_gate, tri_out,
        att_project, att_bias, att_out,
    )
    return pair_out.reshape(pair_rep.shape)


def solution(mesh):
    return jax.shard_map(
        local,
        mesh=mesh,
        in_specs=(P("row", "col", None), P(), P(), P(), P(), P(), P(), P(), P(), P()),
        out_specs=P("row", "col", None),
        check_vma=False,
    )
```

```python
import jax
import jax.numpy as jnp
from jax import lax
from jax.sharding import PartitionSpec as P
from jax.experimental import pallas as pl
from jax.experimental.pallas import tpu as pltpu

F32 = jnp.float32
BF16 = jnp.bfloat16
MESH = pl.DeviceIdType.MESH
CZ = 128
ROWS, COLS = 8, 16
IL, JL = 48, 24
PX = IL * JL
NRES = 384
QS = PX // 128
PARTS = 3
HEADS, DH = 4, 32
STRIP = 3 * JL
LINE0 = 80
LOG2E = 1.4426950408889634
SCALE = DH ** -0.5


def normalize(v):
    mean = jnp.mean(v, axis=-1, keepdims=True)
    c = v - mean
    spread = jnp.mean(c * c, axis=-1, keepdims=True)
    return c * lax.rsqrt(spread + 1e-05)


def sigmoid(v):
    return 0.5 * jnp.tanh(0.5 * v) + 0.5


def dot(a, b, dims=((1,), (0,))):
    return lax.dot_general(a, b, (dims, ((), ())), preferred_element_type=F32)


def repeat(n, body, first=0, unroll=1):
    def step(i, carry):
        body(i)
        return carry

    lax.fori_loop(first, n, step, 0, unroll=unroll)


def to_peers(axis, r, s, act):
    n, me = (ROWS, r) if axis == "row" else (COLS, s)

    def one(d):
        p = jnp.bitwise_xor(me, n - d)
        act(p, (p, s) if axis == "row" else (r, p))

    repeat(n, one, 1, 7 if n == ROWS else 5)


def scatter_to(axis, src, dst, send, recv, r, s):
    to_peers(axis, r, s, lambda p, device: pltpu.make_async_remote_copy(
        src_ref=src(p), dst_ref=dst, send_sem=send, recv_sem=recv, device_id=device, device_id_type=MESH
    ).start())


def drain(ref, sem):
    pltpu.make_async_copy(ref, ref, sem).wait()


def three(a):
    return pl.ds(3 * a, 3)


class Triangle:
    SHAPES = [
        ((ROWS, QS, 32, 128), BF16), ((ROWS, QS, 32, 128), BF16),
        ((COLS, QS, 16, 128), BF16), ((COLS, QS, 16, 128), BF16),
        ((COLS, PARTS, 32, 128), BF16), ((COLS, PARTS, 32, 128), BF16),
        ((ROWS, QS, 16, 128), BF16), ((ROWS, QS, 16, 128), BF16),
    ]

    def __init__(self, t, x, nb, mask, weights, bufs, stage, left, right, sends, recvs, r, s):
        self.t, self.x, self.nb, self.mask, self.r, self.s = t, x, nb, mask, r, s
        self.proj, self.gate, self.out = weights
        self.s1, self.r1, self.s2, self.r2, self.s3, self.r3, self.s4, self.r4 = bufs
        self.stage, self.left, self.right, self.sends, self.recvs = stage, left, right, sends, recvs

    def side(self, a):

        def chunk(i, _):
            q = 3 * a + i
            rows = pl.ds(pl.multiple_of(q * 128, 128), 128)
            n = normalize(self.x[rows, :]).astype(BF16)
            self.nb[rows, :] = n
            p = dot(n, self.proj[self.t])
            m = self.mask[pl.ds(q, 1), :]
            for k in range(2):
                v = sigmoid(p[:, (2 * k + 1) * CZ:(2 * k + 2) * CZ]) * p[:, 2 * k * CZ:(2 * k + 1) * CZ]
                v = (v.T * m).astype(BF16)
                for p_ in range(ROWS):
                    self.s1[p_, q, 16 * k:16 * k + 16, :] = v[16 * p_:16 * p_ + 16]
            return 0

        lax.fori_loop(0, 3, chunk, 0, unroll=3)

    def side_out(self, a):
        r, s = self.r, self.s
        scatter_to("row", lambda p: self.s1.at[p, three(a)], self.r1.at[r, three(a)], self.sends.at[0], self.recvs.at[0, a], r, s)
        self.r1[r, three(a)] = self.s1[r, three(a)]

    def relay(self, a):
        r, s, mid = self.r, self.s, self.stage
        drain(self.r1.at[pl.ds(0, ROWS - 1), three(a)], self.recvs.at[0, a])

        def chunk(i, _):
            q = 3 * a + i
            for p in range(ROWS):
                v = self.r1[p, q].astype(F32)
                for k in range(2):
                    mid[pl.ds(i * 256 + k * 8 + p, 16, stride=16), :] = v[16 * k:16 * k + 16]
            for c in range(16):
                self.s2[c, q] = mid[pl.ds(pl.multiple_of(i * 256 + c * 16, 16), 16), :].astype(BF16)
            return 0

        lax.fori_loop(0, 3, chunk, 0, unroll=3)
        scatter_to("col", lambda p: self.s2.at[p, three(a)], self.r2.at[s, three(a)], self.sends.at[1], self.recvs.at[1, a], r, s)
        self.r2[s, three(a)] = self.s2[s, three(a)]

    def gather(self, a):
        f = self.stage
        drain(self.r2.at[pl.ds(0, COLS - 1), three(a)], self.recvs.at[1, a])
        for i in range(3):
            for p in range(COLS):
                f[i * 256 + p * 16:i * 256 + p * 16 + 16, :] = self.r2[p, 3 * a + i].astype(F32)
        for k, ref in enumerate((self.left, self.right)):
            v = [jnp.concatenate([f[pl.ds(i * 256 + k * 8 + p, COLS, stride=16), :] for i in range(3)], axis=1) for p in range(ROWS)]
            for b in range(8):
                row = jnp.concatenate([u[:, IL * b:IL * (b + 1)] for u in v], axis=1)
                for i in range(3):
                    ref[pl.ds(i * NRES + 8 * a + b, COLS, stride=JL), :] = row[:, 128 * i:128 * (i + 1)]

    def multiply(self):
        lf, rt = (jnp.concatenate([ref[pl.ds(i * NRES, NRES), :] for i in range(3)], axis=1).astype(BF16) for ref in (self.left, self.right))
        prod = dot(rt, lf, ((0,), (0,))) if self.t == 0 else dot(rt, lf, ((1,), (1,)))
        for i in range(3):
            self.left[pl.ds(i * NRES, NRES), :] = prod[:, 128 * i:128 * (i + 1)]

    def give(self, a):
        r, s = self.r, self.s
        for p in range(COLS):
            v = [self.left[pl.ds(i * NRES + JL * p + 8 * a, 8), :] for i in range(3)]
            self.s3[p, a] = jnp.concatenate(v + [jnp.zeros((8, 128), F32)], axis=0).astype(BF16)
        scatter_to("col", lambda p: self.s3.at[p, a], self.r3.at[s, a], self.sends.at[2], self.recvs.at[2, a], r, s)
        self.r3[s, a] = self.s3[s, a]

    def relay_back(self, a):
        r, s, f = self.r, self.s, self.stage
        drain(self.r3.at[pl.ds(0, COLS - 1), a], self.recvs.at[2, a])
        for c in range(COLS):
            f[c * 32:c * 32 + 32, :] = self.r3[c, a].astype(F32)
        v = [jnp.concatenate([f[pl.ds(i * 8 + b, 16, stride=32), :] for i in range(3)], axis=1) for b in range(8)]
        for p in range(ROWS):
            row = jnp.concatenate([u[:, IL * p:IL * (p + 1)] for u in v], axis=1).astype(BF16)
            for i in range(3):
                self.s4[p, 3 * a + i] = row[:, 128 * i:128 * (i + 1)]
        scatter_to("row", lambda p: self.s4.at[p, three(a)], self.r4.at[r, three(a)], self.sends.at[3], self.recvs.at[3, a], r, s)
        self.r4[r, three(a)] = self.s4[r, three(a)]

    def finish(self, a):
        drain(self.r4.at[pl.ds(0, ROWS - 1), three(a)], self.recvs.at[3, a])

        def chunk(i, _):
            q = 3 * a + i
            rows = pl.ds(pl.multiple_of(q * 128, 128), 128)
            pr = jnp.concatenate([self.r4[p, q] for p in range(ROWS)], axis=0).astype(F32).T
            mixed = normalize(pr).astype(BF16)
            g = sigmoid(dot(self.nb[rows, :], self.gate[self.t]))
            self.x[rows, :] = self.x[rows, :] + g * dot(mixed, self.out[self.t])
            return 0

        lax.fori_loop(0, 3, chunk, 0, unroll=3)

    def middle(self):
        for step in (self.relay, self.gather):
            repeat(PARTS, step)
        self.multiply()
        for step in (self.give, self.relay_back):
            repeat(PARTS, step)

    def close(self):
        drain(self.s1.at[pl.ds(0, ROWS - 1)], self.sends.at[0])
        drain(self.s2.at[pl.ds(0, COLS - 1)], self.sends.at[1])
        drain(self.s3.at[pl.ds(0, COLS - 1)], self.sends.at[2])
        drain(self.s4.at[pl.ds(0, ROWS - 1)], self.sends.at[3])


class Attention:
    @staticmethod
    def shapes(t):
        msg = (COLS, LINE0, CZ) if t == 0 else (ROWS, 3 * IL, CZ)
        return [((ROWS, QS, HEADS, 128), F32), ((COLS * HEADS * STRIP, 128), F32)] + [(msg, BF16)] * 4

    SHARED = [
        ((PX, CZ), F32), ((PX, CZ), F32), ((PX, CZ), BF16), ((PX, CZ), BF16), ((PX, CZ), BF16), ((PX, CZ), F32),
        ((3 * CZ, NRES), BF16), ((PX, CZ), F32), ((3 * CZ, NRES), F32), ((PX, CZ), F32),
    ]

    def __init__(self, t, x, kb, weights, bufs, shared, sems, slots, r, s):
        self.t, self.x, self.kb, self.sems, self.slots, self.r, self.s = t, x, kb, sems, slots, r, s
        self.bias_w, self.w_project, self.w_out = weights
        self.p1, self.bias, self.msg, self.got, self.upd, self.back = bufs
        self.nf, self.line, self.qs, self.ks, self.vs, self.gs, self.vt, self.us, self.ot, self.acc = shared

    def chunk(self, a):
        t, r, s = self.t, self.r, self.s

        def one(i, _):
            q = 3 * a + i
            rows = pl.ds(pl.multiple_of(q * 128, 128), 128)
            n = normalize(self.x[rows, :])
            self.nf[rows, :] = n
            b8 = lax.dot_general(self.bias_w[t], n, (((1,), (1,)), ((), ())), precision=lax.Precision.HIGHEST, preferred_element_type=F32)
            self.p1[r, q] = (b8[:HEADS] + self.kb[t, pl.ds(q, 1), :]) * LOG2E
            return 0

        lax.fori_loop(0, 3, one, 0, unroll=3)
        mine = self.p1.at[r, three(a)]
        scatter_to("row", lambda p: mine, mine, self.sems.at[0], self.sems.at[4 + a], r, s)

    def at(self, dx, dy, dc):
        x, y, c = self.s // 8, (self.s % 8) // 2, self.s % 2
        return ((x + dx) % 2) * 8 + ((y + dy) % 4) * 2 + (c + dc) % 2

    def piece(self, slot, h):
        return self.bias.at[pl.ds(pl.multiple_of((slot * HEADS + h) * STRIP, 8), STRIP)]

    def arrived(self, d, h):
        drain(self.piece(self.at(*d), h), self.slots.at[self.at(*d), h])

    def pass_on(self, d, h, *targets):
        slot = self.at(*d)
        for target in targets:
            pltpu.make_async_remote_copy(
                src_ref=self.piece(slot, h), dst_ref=self.piece(slot, h), send_sem=self.sems.at[2], recv_sem=self.slots.at[slot, h],
                device_id=(self.r, self.at(*target)), device_id_type=MESH,
            ).start()

    def forward(self, h, step):
        across, up, down, other = (1, 0, 0), (0, 1, 0), (0, 3, 0), (0, 0, 1)
        if step == 0:
            self.arrived(up, h)
            self.pass_on(up, h, other)
            self.arrived(down, h)
            self.pass_on(down, h, other)
            pl.when(h < 2)(lambda: self.pass_on(up, h, down))
            pl.when(h >= 2)(lambda: self.pass_on(down, h, up))
            self.arrived(across, h)
            self.pass_on(across, h, up, down, other)
        elif step == 1:
            self.arrived((0, 2, 0), h)
            self.pass_on((0, 2, 0), h, across, other)
            for d in ((1, 1, 0), (1, 3, 0)):
                self.arrived(d, h)
                self.pass_on(d, h, other)
        elif step == 2:
            self.arrived((1, 2, 0), h)
            self.pass_on((1, 2, 0), h, other)
        else:
            repeat(8, lambda n: self.arrived((n // 4, n % 4, 1), h))

    def lines_out(self):
        if self.t == 0:
            for p in range(COLS):
                v = [self.nf[pl.ds(3 * p + u, JL, stride=IL), :] for u in range(3)]
                self.msg[p] = jnp.concatenate(v + [jnp.zeros((LINE0 - 72, CZ), F32)], axis=0).astype(BF16)
        else:
            for p in range(ROWS):
                self.msg[p] = self.nf[pl.ds(p * 3 * IL, 3 * IL), :].astype(BF16)
        scatter_to(self.axis(), lambda p: self.msg.at[p], self.got.at[self.me()], self.sems.at[1], self.sems.at[7], self.r, self.s)
        self.got[self.me()] = self.msg[self.me()]

    def axis(self):
        return "col" if self.t == 0 else "row"

    def me(self):
        return self.s if self.t == 0 else self.r

    def others(self):
        return pl.ds(0, COLS - 1 if self.t == 0 else ROWS - 1)

    def lines_in(self):
        drain(self.got.at[self.others()], self.sems.at[7])
        if self.t == 0:
            for p in range(COLS):
                v = self.got[p].astype(F32)
                for u in range(3):
                    self.line[pl.ds(u * NRES + p * JL, JL), :] = v[u * JL:(u + 1) * JL]
        else:
            for p in range(ROWS):
                for u in range(3):
                    self.line[pl.ds(u * NRES + p * IL, IL), :] = self.got[p, u * IL:(u + 1) * IL, :].astype(F32)

    def lay(self, a):
        drain(self.p1.at[pl.ds(0, ROWS - 1), three(a)], self.sems.at[4 + a])
        v = [jnp.concatenate([self.p1[p, 3 * a + i] for i in range(3)], axis=1) for p in range(ROWS)]
        for b in range(8):
            row = jnp.concatenate([u[:, IL * b:IL * (b + 1)] for u in v], axis=1)
            for i in range(3):
                self.bias[pl.ds(self.s * HEADS * STRIP + i * JL + 8 * a + b, HEADS, stride=STRIP), :] = row[:, 128 * i:128 * (i + 1)]

    def project(self, u):
        rows = pl.ds(u * NRES, NRES)
        p = dot(self.line[rows, :].astype(BF16), self.w_project[self.t])
        self.qs[rows, :] = p[:, :CZ].astype(BF16)
        self.ks[rows, :] = p[:, CZ:2 * CZ].astype(BF16)
        v = p[:, 2 * CZ:3 * CZ]
        if self.t == 0:
            self.vt[pl.ds(u * CZ, CZ), :] = v.T.astype(BF16)
        else:
            self.vs[rows, :] = v.astype(BF16)
        self.gs[rows, :] = sigmoid(p[:, 3 * CZ:])

    def weights_of(self, scores, bias):
        e = scores * (SCALE * LOG2E) + bias
        return jnp.exp2(e - jnp.max(e, axis=self.t, keepdims=True))

    def bias_rows(self, slot, h, i):
        return self.bias[pl.ds(pl.multiple_of((slot * HEADS + h) * STRIP + i * JL, 8), JL), :]

    def tile(self, u, h):
        keep = lax.broadcasted_iota(jnp.int32, (1, CZ), 1) // DH == h
        k = self.ks[pl.ds(u * NRES, NRES), :]
        if self.t == 0:
            vt = self.vt[pl.ds(pl.multiple_of(u * CZ + h * DH, DH), DH), :]
            for i in range(3):
                q = self.qs[pl.ds(u * NRES + i * 128, 128), :]
                q = jnp.where(keep, q, jnp.zeros_like(q))
                b = jnp.concatenate([self.bias_rows(p, h, i) for p in range(COLS)], axis=0)
                e = self.weights_of(dot(k, q, ((1,), (1,))), b)
                o = dot(vt, e.astype(BF16)) / jnp.sum(e, axis=0, keepdims=True)
                self.ot[pl.ds(pl.multiple_of(u * CZ + h * DH, DH), DH), pl.ds(i * 128, 128)] = o
        else:
            v = self.vs[pl.ds(u * NRES, NRES), :]
            k = jnp.where(keep, k, jnp.zeros_like(k))
            v = jnp.concatenate([jnp.where(keep, v, jnp.zeros_like(v)), jnp.ones_like(v)], axis=1)
            for i in range(4):
                rows = pl.ds(u * NRES + i * 96, 96)
                b = jnp.concatenate([
                    jnp.concatenate([self.bias_rows(4 * i + p, h, w) for p in range(4)], axis=0) for w in range(3)], axis=1)
                e = self.weights_of(dot(self.qs[rows, :], k, ((1,), (1,))), b)
                o = dot(e.astype(BF16), v)
                o = o[:, :CZ] / o[:, CZ:]
                self.acc[rows, :] = self.acc[rows, :] + o

    def merge(self, u):
        rows = pl.ds(u * NRES, NRES)
        att = self.ot[pl.ds(u * CZ, CZ), :].T if self.t == 0 else self.acc[rows, :]
        self.us[rows, :] = dot((self.gs[rows, :] * att).astype(BF16), self.w_out[self.t])

    def run(self):
        self.lines_out()
        repeat(PARTS, self.lay)
        repeat(HEADS, lambda h: self.pass_on((0, 0, 0), h, (0, 1, 0), (0, 3, 0), (1, 0, 0), (0, 0, 1)))
        self.lines_in()
        if self.t == 1:
            self.acc[...] = jnp.zeros_like(self.acc)
        for u in range(3):
            self.project(u)

        def head(turn):
            for step in range(3):
                h = turn - step
                pl.when((h >= 0) & (h < HEADS))(lambda: self.forward(h, step))

            @pl.when(turn >= 3)
            def _():
                self.forward(turn - 3, 3)
                for u in range(3):
                    self.tile(u, turn - 3)

        repeat(HEADS + 3, head)
        for u in range(3):
            self.merge(u)
        if self.t == 0:
            for p in range(COLS):
                v = [self.us[pl.ds(u * NRES + p * JL, JL), :] for u in range(3)]
                self.upd[p] = jnp.concatenate(v + [jnp.zeros((LINE0 - 72, CZ), F32)], axis=0).astype(BF16)
        else:
            for p in range(ROWS):
                for u in range(3):
                    self.upd[p, u * IL:(u + 1) * IL, :] = self.us[pl.ds(u * NRES + p * IL, IL), :].astype(BF16)
        scatter_to(self.axis(), lambda p: self.upd.at[p], self.back.at[self.me()], self.sems.at[3], self.sems.at[8], self.r, self.s)
        self.back[self.me()] = self.upd[self.me()]
        drain(self.back.at[self.others()], self.sems.at[8])
        if self.t == 0:
            for p in range(COLS):
                v = self.back[p].astype(F32)
                for u in range(3):
                    rows = pl.ds(3 * p + u, JL, stride=IL)
                    self.x[rows, :] = self.x[rows, :] + v[u * JL:(u + 1) * JL]
        else:
            for p in range(ROWS):
                rows = pl.ds(p * 3 * IL, 3 * IL)
                self.x[rows, :] = self.x[rows, :] + self.back[p].astype(F32)

    def close(self):
        drain(self.p1.at[pl.ds(0, ROWS - 1)], self.sems.at[0])
        drain(self.msg.at[self.others()], self.sems.at[1])
        drain(self.bias.at[pl.ds(0, 15 * HEADS * STRIP)], self.sems.at[2])
        drain(self.upd.at[self.others()], self.sems.at[3])


def kernel(pair, chain, live, table, proj, gate, out, att_w, bias_c, att_o, y, x, nb, mask, kb, bias_w, stage, left, right, *more):
    r = lax.axis_index("row")
    s = lax.axis_index("col")
    barrier = pltpu.get_barrier_semaphore()
    for axis in ("row", "col"):
        to_peers(axis, r, s, lambda _, device: pl.semaphore_signal(barrier, inc=1, device_id=device, device_id_type=MESH))

    first, second = (r * IL).astype(F32), (s * JL).astype(F32)
    live_count = jnp.sum(live[...].reshape(1, NRES).astype(F32), axis=1, keepdims=True)
    begins = [jnp.sum((chain[...].reshape(1, NRES) < c).astype(F32), axis=1, keepdims=True) for c in (1, 2, 3)]

    def chain_of(residue):
        return sum((residue >= b).astype(F32) for b in begins)

    px = (lax.broadcasted_iota(jnp.int32, (QS, 128), 0) * 128 + lax.broadcasted_iota(jnp.int32, (QS, 128), 1)).astype(F32)
    jl = jnp.floor((px + 0.5) * (1.0 / IL))
    live_i = (first + px - IL * jl < live_count).astype(F32)
    live_j = (second + jl < live_count).astype(F32)
    mask[...] = live_i * live_j
    kb[0] = (live_j - 1.0) * 1e9
    kb[1] = (live_i - 1.0) * 1e9
    for t in range(2):
        wide = jnp.concatenate([bias_c[t], jnp.zeros((CZ, 128 - HEADS), F32)], axis=1)
        bias_w[t] = wide.T[:8]
    chain_i = chain_of(first + lax.broadcasted_iota(jnp.int32, (IL, CZ), 0).astype(F32))
    for j in range(JL):
        same = chain_i == chain_of(second + jnp.full((1, CZ), j, F32))
        x[pl.ds(j * IL, IL), :] = pair[pl.ds(j, IL, stride=JL), :] + jnp.where(same, table[1:2, :], table[0:1, :])

    more = list(more)

    def take(n):
        got, more[:] = more[:n], more[n:]
        return got

    tri_bufs = [take(8), take(8)]
    att_bufs = [take(6), take(6)]
    shared = take(len(Attention.SHARED))
    tri_send, tri_recv, att_sems, slots = take(4)
    tri = [Triangle(t, x, nb, mask, (proj, gate, out), tri_bufs[t], stage, left, right, tri_send.at[t], tri_recv.at[t], r, s) for t in range(2)]
    att = [Attention(t, x, kb, (bias_w, att_w, att_o), att_bufs[t], shared, att_sems.at[t], slots.at[t], r, s) for t in range(2)]

    tri[0].side(0)
    pl.semaphore_wait(barrier, ROWS + COLS - 2)
    tri[0].side_out(0)
    repeat(PARTS, lambda a: (tri[0].side(a), tri[0].side_out(a)), 1)
    tri[0].middle()
    repeat(PARTS, lambda a: (tri[0].finish(a), tri[1].side(a), tri[1].side_out(a)))
    tri[1].middle()
    repeat(PARTS, lambda a: (tri[1].finish(a), att[0].chunk(a)))
    att[0].run()
    repeat(PARTS, att[1].chunk)
    att[1].run()
    for j in range(JL):
        y[pl.ds(j, IL, stride=JL), :] = x[pl.ds(j * IL, IL), :]
    for part in tri + att:
        part.close()


def call(*args):
    vm = pl.BlockSpec(memory_space=pltpu.VMEM)
    shapes = [
        ((PX, CZ), F32), ((PX, CZ), BF16), ((QS, 128), F32), ((2, QS, 128), F32), ((2, 8, CZ), F32), ((3 * 256, 128), F32), ((3 * NRES, 128), F32),
        ((3 * NRES, 128), F32), *Triangle.SHAPES, *Triangle.SHAPES, *Attention.shapes(0), *Attention.shapes(1), *Attention.SHARED,
    ]
    return pl.pallas_call(
        kernel,
        out_shape=jax.ShapeDtypeStruct((PX, CZ), F32),
        in_specs=[vm] * len(args),
        out_specs=vm,
        scratch_shapes=[pltpu.VMEM(*shape) for shape in shapes] + [
            pltpu.SemaphoreType.DMA((2, 4)),
            pltpu.SemaphoreType.DMA((2, 4, PARTS)),
            pltpu.SemaphoreType.DMA((2, 9)),
            pltpu.SemaphoreType.DMA((2, COLS, HEADS)),
        ],
        compiler_params=pltpu.CompilerParams(collective_id=0, has_side_effects=True, vmem_limit_bytes=56 << 20),
    )(*args)


def local(pair_rep, chain_id, live_mask, chain_table, tri_proj, tri_gate, tri_out, att_project, att_bias, att_out):
    pair_out = call(
        pair_rep.reshape(PX, CZ), chain_id, live_mask, chain_table, tri_proj, tri_gate, tri_out,
        att_project, att_bias, att_out,
    )
    return pair_out.reshape(pair_rep.shape)


def solution(mesh):
    return jax.shard_map(
        local,
        mesh=mesh,
        in_specs=(P("row", "col", None), P(), P(), P(), P(), P(), P(), P(), P(), P()),
        out_specs=P("row", "col", None),
        check_vma=False,
    )
```
